512 devices in a mesh: pool: 64 (over z, y), tensor: 8 (over x, core).
Axes of the slice: x: 4, y: 8, z: 8, core: 2. Of those that a mesh axis runs over, the one named last changes fastest.
Arguments:
- stream: bfloat16 [16, 8192], P(None, 'pool'), may hold values from -72 to 72, as said below
- norm_gain: bfloat16 [8192], P('pool'), may hold values from 0.099609375 to 1.8984375
- query_weight: bfloat16 [8192, 8192], P('pool', 'tensor'), may hold values from -0.0625 to 0.0625
- query_bias: bfloat16 [8192], P('tensor'), may hold values from -2.5 to 2.5
- key_matrix: bfloat16 [8192, 1024], P('pool', 'tensor'), may hold values from -0.0625 to 0.0625
- key_offset_bias: bfloat16 [1024], P('tensor'), may hold values from -2.5 to 2.5
- value_matrix: bfloat16 [8192, 1024], P('pool', 'tensor'), may hold values from -0.0625 to 0.0625
- value_offset_bias: bfloat16 [1024], P('tensor'), may hold values from -2.5 to 2.5
- out_weight: bfloat16 [8192, 8192], P('tensor', 'pool'), may hold values from -0.0625 to 0.0625
- key_pages: bfloat16 [1024, 128, 8, 128], P('pool', None, 'tensor'), may hold values from -52 to 52, as said below
- paged_values: bfloat16 [1024, 128, 8, 128], P('pool', None, 'tensor'), may hold values from -4 to 4
- block_table: int32 [16, 256], replicated, may hold values from -1 to 1023, as said below
- lengths: int32 [16], replicated, may hold values from 1 to 32768, as said below
Outputs:
- branch: bfloat16 [2, 16, 8192], P(None, None, 'pool')
- appended: bfloat16 [2, 2, 16, 8, 128], P(None, None, None, 'tensor')
The draws below stay inside these ranges and needn't reach their ends.
Inputs may be any that keep to these rules, and one draw needn't show every extreme that they name: The stream rows and columns have different scales. `key_pages`: cached keys are real-valued. `lengths`: one sequence holds exactly 32768 tokens; the others hold at most 4096. block_table[s, j] names the page holding tokens j * 128 to j * 128 + 127 of sequence s for j below ceil(lengths[s] / 128), and is -1 beyond; no page is named twice; page p is held by pool index p // 16; pool indices hold unequal numbers of named pages.
All inputs are finite; a program needn't handle non-finite values.
Results may differ from the reference program's by a relative error of at most 0.03.
Values may be sent and summed in bfloat16 or wider, within the bound.
A program may use at most 64 MiB of HBM per device.

```python
import math
import jax
import jax.numpy as jnp
from jax import lax

MODEL_WIDTH = 8192
QUERY_HEADS = 64
KEY_VALUE_HEADS = 8
HEAD_SIZE = 128
PAGE_TOKENS = 128
DECODE_SEQUENCES = 16
PAGES_DEV = 16
MAXBLK = 256
PAGE_SLOTS = 1024


def table_layout(key):
    length_key, weight_key, score_key = jax.random.split(key, 3)
    longest = jax.random.randint(length_key, (), 0, DECODE_SEQUENCES)
    shorter = jax.random.randint(jax.random.fold_in(length_key, 1), (DECODE_SEQUENCES,), 1, MAXBLK // 8 * PAGE_TOKENS + 1)
    context = jnp.where(jnp.arange(DECODE_SEQUENCES) == longest, MAXBLK * PAGE_TOKENS, shorter).astype(jnp.int32)
    blocks = (context + PAGE_TOKENS - 1) // PAGE_TOKENS
    finish = jnp.cumsum(blocks)
    begins = finish - blocks
    shard_weight = jax.random.randint(weight_key, (PAGE_SLOTS // PAGES_DEV,), 1, 5)
    shard_of = jnp.arange(PAGE_SLOTS, dtype=jnp.int32) // PAGES_DEV
    ranked = jax.random.randint(score_key, (PAGE_SLOTS,), 0, 4096) * shard_weight[shard_of]
    ranking = jnp.argsort(ranked * PAGE_SLOTS + jnp.arange(PAGE_SLOTS, dtype=jnp.int32)).astype(jnp.int32)
    column = jnp.arange(MAXBLK, dtype=jnp.int32)
    flat_index = jnp.minimum(begins[:, None] + column[None, :], PAGE_SLOTS - 1)
    page_table = jnp.where(column[None, :] < blocks[:, None], ranking[flat_index], -1).astype(jnp.int32)
    return (context, page_table)


def draw_lengths(key, part):
    return table_layout(key)[0]


def draw_block_table(key, part):
    return table_layout(key)[1]


def draw_stream(key, part):
    key = jax.random.fold_in(key, 3)
    row_key, column_key, value_key = jax.random.split(key, 3)
    row_scale = jnp.exp(jax.random.uniform(row_key, (DECODE_SEQUENCES, 1), jnp.float32, -1.2, 1.1))
    column_scale = jnp.exp(1.0986 * jnp.arange(MODEL_WIDTH, dtype=jnp.float32)[None, :] / MODEL_WIDTH + jax.random.uniform(column_key, (1, MODEL_WIDTH), jnp.float32, -0.5, 0.5))
    entries = jnp.clip(jax.random.normal(value_key, (DECODE_SEQUENCES, MODEL_WIDTH), jnp.float32), -4.0, 4.0)
    return (entries * row_scale * column_scale).astype(jnp.bfloat16)


def draw_key_pages(key, part):
    key = jax.random.fold_in(key, 7)
    base_key = jax.random.fold_in(key, 0)
    page_layout = (PAGE_SLOTS, PAGE_TOKENS, KEY_VALUE_HEADS, HEAD_SIZE)
    drawn = jnp.clip(jax.random.normal(base_key, page_layout, jnp.float32), -4.0, 4.0)
    return drawn.astype(jnp.bfloat16)


def level_of(rng, extent, cuts, low, largest):
    level, own = 1.0, jax.random.fold_in(rng, 6)
    for dim, shards_of in cuts:
        heights = jnp.exp(jax.random.uniform(jax.random.fold_in(own, dim), (shards_of,), jnp.float32, low / len(cuts), largest / len(cuts)))
        level = level * jnp.repeat(heights, extent[dim] // shards_of).reshape([-1 if axis == dim else 1 for axis in range(len(extent))])
    return level


def centred(key, extent, scale, most, pieces=(), kind=jnp.bfloat16):
    values = scale * jax.random.normal(key, extent, jnp.float32)
    if pieces:
        values = values * level_of(key, extent, pieces, -0.22, 0.18)
    return jnp.clip(values, -most, most).astype(kind)


def setup_inputs(seed: int = 0) -> dict:
    key_of = jax.random.split(jax.random.key(seed), 14)
    return {
        "stream": draw_stream(jax.random.fold_in(key_of[13], 71), 0),
        "norm_gain": jnp.clip(1.0 + 0.18 * jax.random.normal(key_of[1], (MODEL_WIDTH,), jnp.float32), 0.099609375, 1.8984375).astype(jnp.bfloat16),
        "query_weight": centred(key_of[2], (MODEL_WIDTH, QUERY_HEADS * HEAD_SIZE), MODEL_WIDTH ** -0.5, 0.0625, ((0, 64), (1, 8))),
        "query_bias": centred(key_of[3], (QUERY_HEADS * HEAD_SIZE,), 0.5, 2.5, ((0, 8),)),
        "key_matrix": centred(key_of[4], (MODEL_WIDTH, KEY_VALUE_HEADS * HEAD_SIZE), MODEL_WIDTH ** -0.5, 0.0625, ((0, 64), (1, 8))),
        "key_offset_bias": centred(key_of[5], (KEY_VALUE_HEADS * HEAD_SIZE,), 0.5, 2.5, ((0, 8),)),
        "value_matrix": centred(key_of[6], (MODEL_WIDTH, KEY_VALUE_HEADS * HEAD_SIZE), MODEL_WIDTH ** -0.5, 0.0625, ((0, 64), (1, 8))),
        "value_offset_bias": centred(key_of[7], (KEY_VALUE_HEADS * HEAD_SIZE,), 0.5, 2.5, ((0, 8),)),
        "out_weight": centred(key_of[8], (QUERY_HEADS * HEAD_SIZE, MODEL_WIDTH), (QUERY_HEADS * HEAD_SIZE) ** -0.5, 0.0625, ((0, 8), (1, 64))),
        "key_pages": draw_key_pages(jax.random.fold_in(key_of[13], 71), 0),
        "paged_values": centred(key_of[10], (PAGE_SLOTS, PAGE_TOKENS, KEY_VALUE_HEADS, HEAD_SIZE), 1.0, 4.0, ((0, 64), (2, 8))),
        "block_table": draw_block_table(jax.random.fold_in(key_of[13], 71), 0),
        "lengths": draw_lengths(jax.random.fold_in(key_of[13], 71), 0),
    }


EPS = 1e-06
NEG = -1e+30

def merge_terms(first, second):
    first_peak, first_total, first_mixed = first
    second_peak, second_total, second_mixed = second
    peak_max = jnp.maximum(first_peak, second_peak)
    first_factor = jnp.exp(first_peak - peak_max)
    second_factor = jnp.exp(second_peak - peak_max)
    return (peak_max, first_total * first_factor + second_total * second_factor, first_mixed * first_factor[..., None] + second_mixed * second_factor[..., None])

def project(current, norm_gain, pairs):
    widened = current.astype(jnp.float32)
    scaled = (widened * norm_gain.astype(jnp.float32)).astype(jnp.bfloat16)
    inverse = lax.rsqrt(lax.optimization_barrier(jnp.sum(widened * widened, axis=1, keepdims=True)) / MODEL_WIDTH + EPS)
    results = []
    for matrix, offset in pairs:
        product = jnp.dot(scaled, matrix, preferred_element_type=jnp.float32)
        results.append((inverse * product + offset.astype(jnp.float32)).astype(jnp.bfloat16))
    return results

def cached_terms(heads_of_query, table_row, length, key_pages, paged_values):
    safe_row = jnp.maximum(table_row, 0).astype(jnp.int32)
    cached_keys = jnp.take(key_pages, safe_row, axis=0).astype(jnp.float32)
    cached_values = jnp.take(paged_values, safe_row, axis=0).astype(jnp.float32)
    position = jnp.arange(MAXBLK * PAGE_TOKENS, dtype=jnp.int32).reshape(MAXBLK, PAGE_TOKENS)
    usable = (position < length) & (table_row[:, None] >= 0)
    scores = jnp.einsum('kgd,ptkd->pkgt', heads_of_query.astype(jnp.float32), cached_keys) * (1.0 / math.sqrt(HEAD_SIZE))
    usable_mask = usable[:, None, None, :]
    scores = jnp.where(usable_mask, scores, NEG)
    peaks = lax.optimization_barrier(jnp.max(scores, axis=3))
    weights = jnp.where(usable_mask, jnp.exp(scores - peaks[..., None]), 0.0).astype(jnp.bfloat16)
    weights = lax.optimization_barrier(weights).astype(jnp.float32)
    totals = lax.optimization_barrier(jnp.sum(weights, axis=3))
    mixed = jnp.einsum('pkgt,ptkd->pkgd', weights, cached_values)
    best = lax.optimization_barrier(jnp.max(peaks, axis=0))
    scale_factor = jnp.exp(peaks - best)
    return (best, lax.optimization_barrier(jnp.sum(totals * scale_factor, axis=0)), lax.optimization_barrier(jnp.sum(mixed * scale_factor[..., None], axis=0)))

def reference(stream, norm_gain, query_weight, query_bias, key_matrix, key_offset_bias, value_matrix, value_offset_bias, out_weight, key_pages, paged_values, block_table, lengths):
    query_group = QUERY_HEADS // KEY_VALUE_HEADS
    score_scale = 1.0 / math.sqrt(HEAD_SIZE)
    current = stream
    recent = []
    branches = []
    appended = []

    def per_sequence(record):
        return cached_terms(record[0], record[1], record[2], key_pages, paged_values)
    for step_index in range(2):
        query_vector, latest_key, latest_value = project(current, norm_gain, ((query_weight, query_bias), (key_matrix, key_offset_bias), (value_matrix, value_offset_bias)))
        heads_of_query = query_vector.reshape(DECODE_SEQUENCES, KEY_VALUE_HEADS, query_group, HEAD_SIZE)
        latest_key = latest_key.reshape(DECODE_SEQUENCES, KEY_VALUE_HEADS, HEAD_SIZE)
        latest_value = latest_value.reshape(DECODE_SEQUENCES, KEY_VALUE_HEADS, HEAD_SIZE)
        recent.append((latest_key, latest_value))
        terms = lax.map(per_sequence, (heads_of_query, block_table, lengths))
        for key_per_token, value_per_token in recent:
            score_per_token = jnp.einsum('syou,syu->syo', heads_of_query.astype(jnp.float32), key_per_token.astype(jnp.float32)) * score_scale
            mixed_per_token = jnp.broadcast_to(value_per_token.astype(jnp.float32)[:, :, None, :], (DECODE_SEQUENCES, KEY_VALUE_HEADS, query_group, HEAD_SIZE))
            terms = merge_terms(terms, (score_per_token, jnp.ones_like(score_per_token), mixed_per_token))
        attended = (terms[2] / terms[1][..., None]).astype(jnp.bfloat16).reshape(DECODE_SEQUENCES, QUERY_HEADS * HEAD_SIZE)
        layer_out = jnp.dot(attended, out_weight, preferred_element_type=jnp.float32)
        branches.append(layer_out.astype(jnp.bfloat16))
        appended.append(jnp.stack([latest_key, latest_value]))
        current = (current.astype(jnp.float32) + layer_out).astype(jnp.bfloat16)
    return (jnp.stack(branches), jnp.stack(appended))
```

```python
import functools
import math

import jax
import jax.numpy as jnp
from jax import lax
from jax.experimental import pallas as pl
from jax.experimental.pallas import tpu as pltpu
from jax.sharding import PartitionSpec as P

MESH = pl.DeviceIdType.MESH
EPS = 1e-06
NEG = -1e30
STEPS = 2
SEQS = 16
GROUP = 8
HEAD = 128
HALF = 64
RING = 8
PAGE = 128
SLOTS = 16
LANES = GROUP * SEQS
FAR_FIRST = (4, 3, 5, 2, 6, 1, 7)
BF16 = jnp.bfloat16
F32 = jnp.float32

A1_Y, A1_Z, A1_SQ, A2_Z, A2_Y, A2_SQ, K1, V1, K2, V2 = range(10)
B1_Y, B1_Z, B1_SY, B1_SZ, B2_Z, B2_Y, B2_SZ, B2_SY, C_T = range(10, 19)
EXCHANGES = 19


def dot(a, b):
    return jnp.dot(a, b, preferred_element_type=F32)


def kernel(
    width,
    x_hbm, gain_hbm, wq_hbm, bq_hbm, wk_hbm, bk_hbm, wv_hbm, bv_hbm, wo_hbm, keys_hbm, values_hbm, table_hbm, lengths_ref,
    branch_ref, appended_ref,
    x_ref, gain_ref, wq, bq, wk, bk, wv, bv, wo, keys, values, table,
    values_t, limits, bias_t,
    big, stat, small,
    local_sem, send_sem, recv_sem,
):
    pool, tensor = lax.axis_index("pool"), lax.axis_index("tensor")
    z, y = pool // RING, lax.rem(pool, RING)

    def on_ring(axis, distance):
        if axis == "y":
            return (z * RING + lax.rem(y + distance, RING), tensor)
        if axis == "z":
            return (lax.rem(z + distance, RING) * RING + y, tensor)
        return (pool, lax.rem(tensor + distance, RING))

    place = {"y": y, "z": z, "t": tensor}
    axis_of = {
        A1_Y: "y", A1_Z: "z", A1_SQ: "y", A2_Z: "z", A2_Y: "y", A2_SQ: "z", K1: "y", V1: "z", K2: "z", V2: "y",
        B1_Y: "y", B1_Z: "z", B1_SY: "y", B1_SZ: "z", B2_Z: "z", B2_Y: "y", B2_SZ: "z", B2_SY: "y", C_T: "t",
    }
    big_at = {name: at for at, name in enumerate((A1_Y, A1_Z, A2_Z, A2_Y, B1_Y, B1_Z, B2_Z, B2_Y))}
    stat_at = {name: at for at, name in enumerate((A1_SQ, A2_SQ, B1_SY, B1_SZ, B2_SZ, B2_SY))}
    small_at = {name: at for at, name in enumerate((K1, V1, K2, V2, C_T))}

    def slots(step, name):
        for ref, at in ((big, big_at), (stat, stat_at), (small, small_at)):
            if name in at:
                return ref.at[step, at[name]]

    def fill(step, name, value):
        ref = slots(step, name)
        ref[place[axis_of[name]]] = value.astype(ref.dtype)

    def send(step, *names):
        for distance in FAR_FIRST:
            for name in names:
                own = slots(step, name).at[place[axis_of[name]]]
                pltpu.make_async_remote_copy(
                    src_ref=own, dst_ref=own,
                    send_sem=send_sem.at[step, name], recv_sem=recv_sem.at[step, name],
                    device_id=on_ring(axis_of[name], distance), device_id_type=MESH,
                ).start()

    def others(step, name, sem):
        part = slots(step, name).at[pl.ds(0, RING - 1)]
        pltpu.make_async_copy(part, part, sem.at[step, name]).wait()

    def receive(step, *names):
        for name in names:
            others(step, name, recv_sem)
        return [slots(step, name)[...].astype(F32) for name in names]

    barrier = pltpu.get_barrier_semaphore()
    for axis in ("y", "z", "t"):
        for distance in FAR_FIRST:
            pl.semaphore_signal(barrier, inc=1, device_id=on_ring(axis, distance), device_id_type=MESH)

    pairs = (
        (x_hbm, x_ref), (gain_hbm, gain_ref), (wq_hbm, wq), (wk_hbm, wk), (wv_hbm, wv), (bq_hbm, bq), (bk_hbm, bk),
        (bv_hbm, bv), (table_hbm, table), (values_hbm, values), (keys_hbm, keys), (wo_hbm, wo),
    )
    loads = [pltpu.make_async_copy(src, dst, local_sem.at[at]) for at, (src, dst) in enumerate(pairs)]
    for load in loads:
        load.start()
    for load in loads[:3]:
        load.wait()

    lane = lax.broadcasted_iota(jnp.int32, (1, LANES), 1)
    lane_seq = lax.rem(lane, SEQS)
    own_seq = lax.broadcasted_iota(jnp.int32, (SEQS, LANES), 0) == lane_seq
    scale = 1.0 / math.sqrt(HEAD)

    def tiled(rows):
        return jnp.concatenate([rows] * GROUP, axis=0)

    def project(current):
        scaled = (current * gain_ref[...].astype(F32)).astype(BF16)
        raw = dot(scaled, wq[...])
        raw = jnp.concatenate([raw[:, h * HEAD:(h + 1) * HEAD] for h in range(GROUP)], axis=0)
        squares = jnp.sum(tiled(current * current).T, axis=0, keepdims=True)
        return scaled, raw.T, squares

    def merged(peaks, outs):
        top = peaks[0]
        for i in range(1, len(peaks)):
            top = jnp.maximum(top, peaks[i])
        weights = [jnp.exp(peak - top) for peak in peaks]
        total, out = weights[0], weights[0] * outs[0]
        for weight, part in zip(weights[1:], outs[1:]):
            total = total + weight
            out = out + weight * part
        return top + jnp.log(total), out / total

    current = x_ref[...].astype(F32)
    recent = []
    for step in range(STEPS):
        scaled, raw_t, squares = project(current)
        fill(step, A1_Y, raw_t[:HALF])
        fill(step, A1_Z, raw_t[HALF:])
        fill(step, A1_SQ, squares)
        if step == 0:
            pl.semaphore_wait(barrier, 3 * (RING - 1))
        send(step, A1_Y, A1_Z, A1_SQ)
        if step == 0:
            for load in loads[3:5]:
                load.wait()
        fill(step, K1, dot(scaled, wk[...]))
        fill(step, V1, dot(scaled, wv[...]))
        send(step, K1, V1)

        if step == 0:
            for load in loads[5:10]:
                load.wait()
            bias = jnp.concatenate(
                [jnp.broadcast_to(bq[h:h + 1, :].astype(F32), (SEQS, HEAD)) for h in range(GROUP)], axis=0
            )
            bias_t[...] = bias.T
            length_row = jnp.zeros((1, LANES), jnp.int32)
            for s in range(SEQS):
                length_row = jnp.where(lane_seq == s, lengths_ref[s], length_row)
            table_t = tiled(table[...].astype(F32)).T
            blocks = table_t.shape[0]
            left = length_row.astype(F32) - PAGE * lax.broadcasted_iota(jnp.int32, (blocks, LANES), 0).astype(F32)
            first_page = pool * SLOTS
            for slot in range(SLOTS):
                wanted = (first_page + slot).astype(F32)
                limits[slot:slot + 1, :] = jnp.max(jnp.where(table_t == wanted, left, 0.0), axis=0, keepdims=True)
            for slot in range(SLOTS):
                span = pl.ds(slot * PAGE, PAGE)
                values_t[:, span] = values[span, :].T

        y_parts, z_parts, square_parts = receive(step, A1_Y, A1_Z, A1_SQ)
        fill(step, A2_Z, jnp.sum(y_parts, axis=0))
        fill(step, A2_Y, jnp.sum(z_parts, axis=0))
        fill(step, A2_SQ, jnp.sum(square_parts, axis=0))
        send(step, A2_Z, A2_Y, A2_SQ)
        k_parts, v_parts = receive(step, K1, V1)
        fill(step, K2, jnp.sum(k_parts, axis=0))
        fill(step, V2, jnp.sum(v_parts, axis=0))
        send(step, K2, V2)
        z_parts, y_parts, square_parts = receive(step, A2_Z, A2_Y, A2_SQ)
        inverse = lax.rsqrt(jnp.sum(square_parts, axis=0) / width + EPS)
        raw_t = jnp.concatenate([jnp.sum(z_parts, axis=0), jnp.sum(y_parts, axis=0)], axis=0)
        query_t = (inverse * raw_t + bias_t[...]).astype(BF16)

        if step == 0:
            loads[10].wait()
        scores = (dot(keys[...], query_t) * scale).reshape(SLOTS, PAGE, LANES)
        usable = lax.broadcasted_iota(jnp.int32, scores.shape, 1).astype(F32) < limits[...][:, None, :]
        scores = jnp.where(usable, scores, NEG)
        peak = jnp.max(jnp.max(scores, axis=0), axis=0, keepdims=True)
        weights = jnp.where(usable, jnp.exp(scores - peak[None]), 0.0).astype(BF16)
        total = jnp.sum(jnp.sum(weights.astype(F32), axis=0), axis=0, keepdims=True)
        out_t = dot(values_t[...], weights.reshape(SLOTS * PAGE, LANES))
        some = total > 0.0
        safe = jnp.where(some, total, 1.0)
        log_total = jnp.where(some, peak + jnp.log(safe), NEG)
        out_t = out_t / safe
        fill(step, B1_Y, out_t[:HALF])
        fill(step, B1_Z, out_t[HALF:])
        fill(step, B1_SY, log_total)
        fill(step, B1_SZ, log_total)
        send(step, B1_Y, B1_Z, B1_SY, B1_SZ)

        k_parts, v_parts = receive(step, K2, V2)
        inverse_rows = jnp.broadcast_to(inverse, (LANES, LANES)).T[:SEQS]
        latest_key = (inverse_rows * jnp.sum(k_parts, axis=0) + bk[...].astype(F32)).astype(BF16)
        latest_value = (inverse_rows * jnp.sum(v_parts, axis=0) + bv[...].astype(F32)).astype(BF16)
        appended_ref[step, 0] = latest_key
        appended_ref[step, 1] = latest_value
        recent.append((latest_key, tiled(latest_value.astype(F32)).T))
        new_scores = [
            jnp.sum(jnp.where(own_seq, dot(key, query_t), 0.0), axis=0, keepdims=True) * scale for key, _ in recent
        ]
        new_total, new_out = merged(new_scores, [value for _, value in recent])

        def gather(first, second, first_stat, second_stat):
            one, two, one_stat, two_stat = receive(step, first, second, first_stat, second_stat)
            return (
                [one_stat[i] for i in range(RING)], [one[i] for i in range(RING)],
                [two_stat[i] for i in range(RING)], [two[i] for i in range(RING)],
            )

        one_stat, one, two_stat, two = gather(B1_Y, B1_Z, B1_SY, B1_SZ)
        one_stat, one = merged(one_stat, one)
        two_stat, two = merged(two_stat, two)
        fill(step, B2_Z, one)
        fill(step, B2_Y, two)
        fill(step, B2_SZ, one_stat)
        fill(step, B2_SY, two_stat)
        send(step, B2_Z, B2_Y, B2_SZ, B2_SY)
        one_stat, one, two_stat, two = gather(B2_Z, B2_Y, B2_SZ, B2_SY)
        _, one = merged(one_stat + [new_total], one + [new_out[:HALF]])
        _, two = merged(two_stat + [new_total], two + [new_out[HALF:]])
        attended = jnp.concatenate([one, two], axis=0).T.astype(BF16)
        attended = jnp.concatenate([attended[h * SEQS:(h + 1) * SEQS] for h in range(GROUP)], axis=1)
        if step == 0:
            loads[11].wait()
        fill(step, C_T, dot(attended, wo[...]))
        send(step, C_T)
        (layer_parts,) = receive(step, C_T)
        layer = layer_parts[0]
        for i in range(1, RING):
            layer = layer + layer_parts[i]
        branch_ref[step] = layer.astype(BF16)
        current = (current + layer).astype(BF16).astype(F32)

    for step in range(STEPS):
        for name in range(EXCHANGES):
            others(step, name, send_sem)


def shards(
    stream, norm_gain, query_weight, query_bias, key_matrix, key_offset_bias, value_matrix, value_offset_bias,
    out_weight, key_pages, paged_values, block_table, lengths, *, width,
):
    tokens = SLOTS * PAGE
    operands = (
        stream, norm_gain.reshape(1, HEAD), query_weight, query_bias.reshape(GROUP, HEAD),
        key_matrix, key_offset_bias.reshape(1, HEAD), value_matrix, value_offset_bias.reshape(1, HEAD),
        out_weight, key_pages.reshape(tokens, HEAD), paged_values.reshape(tokens, HEAD), block_table, lengths,
    )
    anywhere = pl.BlockSpec(memory_space=pl.ANY)
    branch, appended = pl.pallas_call(
        functools.partial(kernel, width),
        out_shape=(
            jax.ShapeDtypeStruct((STEPS, SEQS, HEAD), BF16),
            jax.ShapeDtypeStruct((STEPS, 2, SEQS, HEAD), BF16),
        ),
        in_specs=[anywhere] * 12 + [pl.BlockSpec(memory_space=pltpu.SMEM)],
        out_specs=(pl.BlockSpec(memory_space=pltpu.VMEM), pl.BlockSpec(memory_space=pltpu.VMEM)),
        scratch_shapes=[pltpu.VMEM(operand.shape, operand.dtype) for operand in operands[:12]] + [
            pltpu.VMEM((HEAD, tokens), BF16),
            pltpu.VMEM((SLOTS, LANES), F32),
            pltpu.VMEM((HEAD, LANES), F32),
            pltpu.VMEM((STEPS, 8, RING, HALF, LANES), BF16),
            pltpu.VMEM((STEPS, 6, RING, 1, LANES), F32),
            pltpu.VMEM((STEPS, 5, RING, SEQS, HEAD), BF16),
            pltpu.SemaphoreType.DMA((12,)),
            pltpu.SemaphoreType.DMA((STEPS, EXCHANGES)),
            pltpu.SemaphoreType.DMA((STEPS, EXCHANGES)),
        ],
        compiler_params=pltpu.CompilerParams(
            collective_id=0, has_side_effects=True, vmem_limit_bytes=48 * 2**20
        ),
        cost_estimate=pl.CostEstimate(flops=400_000_000, bytes_accessed=2_000_000, transcendentals=600_000),
    )(*operands)
    return branch, appended.reshape(STEPS, 2, SEQS, 1, HEAD)


def solution(mesh):
    in_specs = (
        P(None, "pool"), P("pool"), P("pool", "tensor"), P("tensor"), P("pool", "tensor"), P("tensor"),
        P("pool", "tensor"), P("tensor"), P("tensor", "pool"), P("pool", None, "tensor", None),
        P("pool", None, "tensor", None), P(), P(),
    )
    out_specs = (P(None, None, "pool"), P(None, None, None, "tensor", None))
    width = mesh.shape["pool"] * HEAD
    return jax.shard_map(
        functools.partial(shards, width=width), mesh=mesh, in_specs=in_specs, out_specs=out_specs, check_vma=False
    )
```

```python
import functools
import math

import jax
import jax.numpy as jnp
from jax import lax
from jax.experimental import pallas as pl
from jax.experimental.pallas import tpu as pltpu
from jax.sharding import PartitionSpec as P

MESH = pl.DeviceIdType.MESH
EPS = 1e-06
NEG = -1e30
STEPS = 2
SEQS = 16
GROUP = 8
HEAD = 128
RING = 8
PAGE = 128
SLOTS = 16
LANES = GROUP * SEQS
TOKENS = SLOTS * PAGE
ONES = 16
CHUNK = 256
LOG2E = math.log2(math.e)
FAR_FIRST = (4, 3, 5, 2, 6, 1, 7)
BF16 = jnp.bfloat16
F32 = jnp.float32

PAIRS = 2
ROWS = HEAD // (2 * PAIRS)
RINGS = "yz"
PHASES = ("A1", "A2", "B1", "B2")


def all_streams():
    streams = {}
    for phase in PHASES:
        for chain in range(2 * PAIRS):
            streams[phase, chain] = ("rows", RINGS[(chain + PHASES.index(phase)) % 2])
    for phase, name, ring in (("A1", "k", "y"), ("A1", "v", "z"), ("A2", "k", "z"), ("A2", "v", "y"), ("C", "layer", "t")):
        streams[phase, name] = ("small", ring)
    for phase, name, ring in (
        ("A1", "squares", "y"), ("A2", "squares", "z"),
        ("B1", "first", "y"), ("B1", "second", "z"), ("B2", "first", "z"), ("B2", "second", "y"),
    ):
        streams[phase, name] = ("stat", ring)
    kinds = {"rows": 0, "small": 0, "stat": 0}
    placed = {}
    for at, (key, (kind, ring)) in enumerate(streams.items()):
        placed[key] = (kind, kinds[kind], ring, at)
        kinds[kind] += 1
    return placed, kinds


STREAMS, COUNTS = all_streams()


def dot(a, b):
    return jnp.dot(a, b, preferred_element_type=F32)


def dot_rows(a, b):
    return lax.dot_general(a, b, (((1,), (1,)), ((), ())), preferred_element_type=F32)


def kernel(
    width,
    x_hbm, gain_hbm, wq_hbm, bq_hbm, wk_hbm, bk_hbm, wv_hbm, bv_hbm, wo_hbm, keys_hbm, values_hbm, table_hbm, lengths_ref,
    branch_ref, appended_ref,
    x_ref, gain_ref, wq, bq, wk, bk, wv, bv, wo, keys, values, table,
    values_t, mask, bias_rows, scores_ref, weights_ref,
    big, stat, small,
    local_sem, send_sem, recv_sem,
):
    pool, tensor = lax.axis_index("pool"), lax.axis_index("tensor")
    z, y = pool // RING, lax.rem(pool, RING)

    def on_ring(axis, distance):
        if axis == "y":
            return (z * RING + lax.rem(y + distance, RING), tensor)
        if axis == "z":
            return (lax.rem(z + distance, RING) * RING + y, tensor)
        return (pool, lax.rem(tensor + distance, RING))

    partners = {(axis, distance): on_ring(axis, distance) for axis in "yzt" for distance in FAR_FIRST}
    place = {"y": y, "z": z, "t": tensor}
    homes = {"rows": big, "small": small, "stat": stat}

    def slots(step, key):
        kind, at, _, _ = STREAMS[key]
        return homes[kind].at[step, at]

    def fill(step, key, value):
        ref = slots(step, key)
        ref[place[STREAMS[key][2]]] = value.astype(ref.dtype)

    def send(step, *keys):
        for distance in FAR_FIRST:
            for key in keys:
                _, _, ring, at = STREAMS[key]
                own = slots(step, key).at[place[ring]]
                pltpu.make_async_remote_copy(
                    src_ref=own, dst_ref=own,
                    send_sem=send_sem.at[step, at], recv_sem=recv_sem.at[step, at],
                    device_id=partners[ring, distance], device_id_type=MESH,
                ).start()

    def others(step, key, sem):
        part = slots(step, key).at[pl.ds(0, RING - 1)]
        pltpu.make_async_copy(part, part, sem.at[step, STREAMS[key][3]]).wait()

    def receive(step, key):
        others(step, key, recv_sem)
        ref = slots(step, key)
        return [ref[i].astype(F32) for i in range(RING)]

    barrier = pltpu.get_barrier_semaphore()
    for axes in ("yz", "t"):
        for distance, axis in [(distance, axis) for distance in FAR_FIRST for axis in axes]:
            pl.semaphore_signal(barrier, inc=1, device_id=partners[axis, distance], device_id_type=MESH)

    pairs = (
        (x_hbm, x_ref), (gain_hbm, gain_ref), (wq_hbm, wq), (wk_hbm, wk), (wv_hbm, wv), (bq_hbm, bq), (bk_hbm, bk),
        (bv_hbm, bv), (table_hbm, table), (values_hbm, values), (keys_hbm, keys), (wo_hbm, wo),
    )
    loads = [pltpu.make_async_copy(src, dst, local_sem.at[at]) for at, (src, dst) in enumerate(pairs)]
    for load in loads:
        load.start()
    for load in loads[:3]:
        load.wait()

    lane = lax.broadcasted_iota(jnp.int32, (1, LANES), 1)
    lane_seq = lax.rem(lane, SEQS)
    own_seq = lax.broadcasted_iota(jnp.int32, (SEQS, LANES), 0) == lane_seq
    scale = LOG2E / math.sqrt(HEAD)

    def tiled(rows):
        return jnp.concatenate([rows] * GROUP, axis=0)

    def weigh(peaks):
        top = peaks[0]
        for peak in peaks[1:]:
            top = jnp.maximum(top, peak)
        weights = [jnp.exp2(peak - top) for peak in peaks]
        total = weights[0]
        for weight in weights[1:]:
            total = total + weight
        share = 1.0 / total
        return [weight * share for weight in weights], top + jnp.log(total) * LOG2E

    def blend(weights, parts):
        out = weights[0] * parts[0]
        for weight, part in zip(weights[1:], parts[1:]):
            out = out + weight * part
        return out

    def summed(parts):
        total = parts[0]
        for part in parts[1:]:
            total = total + part
        return total

    chains = range(2 * PAIRS)
    pairs_of = [(2 * p, 2 * p + 1) for p in range(PAIRS)]
    span_of = [slice(c * ROWS, (c + 1) * ROWS) for c in chains]

    current = x_ref[...].astype(F32)
    recent = []
    for step in range(STEPS):
        scaled = (current * gain_ref[...].astype(F32)).astype(BF16)
        raw = dot(scaled, wq[...]).astype(BF16)
        for chain in chains:
            own = slots(step, ("A1", chain))
            for at in range(ROWS // SEQS):
                h = chain * (ROWS // SEQS) + at
                own[place[RINGS[chain % 2]], at * SEQS:(at + 1) * SEQS, :] = raw[:, h * HEAD:(h + 1) * HEAD]
        squares = jnp.sum((current * current).T, axis=0, keepdims=True)
        fill(step, ("A1", "squares"), jnp.concatenate([squares, jnp.ones((1, LANES - SEQS), F32)], axis=1))
        if step == 0:
            pl.semaphore_wait(barrier, 3 * (RING - 1))
        for at, pair in enumerate(pairs_of):
            keys_sent = [("A1", chain) for chain in pair]
            send(step, *(keys_sent + [("A1", "squares")] if at == 0 else keys_sent))
        if step == 0:
            for load in loads[3:5]:
                load.wait()
        fill(step, ("A1", "k"), dot(scaled, wk[...]))
        fill(step, ("A1", "v"), dot(scaled, wv[...]))
        send(step, ("A1", "k"), ("A1", "v"))

        if step == 0:
            for load in loads[5:10]:
                load.wait()
            for h in range(GROUP):
                bias_rows[h * SEQS:(h + 1) * SEQS, :] = jnp.broadcast_to(bq[h:h + 1, :].astype(F32), (SEQS, HEAD))
            length_row = jnp.zeros((1, LANES), jnp.int32)
            for s in range(SEQS):
                length_row = jnp.where(lane_seq == s, lengths_ref[s], length_row)
            table_t = tiled(table[...].astype(F32)).T
            blocks = table_t.shape[0]
            left = length_row.astype(F32) - PAGE * lax.broadcasted_iota(jnp.int32, (blocks, LANES), 0).astype(F32)
            token = lax.broadcasted_iota(jnp.int32, (PAGE, LANES), 0).astype(F32)
            first_page = pool * SLOTS
            for slot in range(SLOTS):
                span = pl.ds(slot * PAGE, PAGE)
                wanted = (first_page + slot).astype(F32)
                limit = jnp.max(jnp.where(table_t == wanted, left, 0.0), axis=0, keepdims=True)
                mask[span, :] = jnp.where(token < limit, 0.0, NEG)
                values_t[:HEAD, span] = values[span, :].T
            values_t[HEAD:, :] = jnp.ones((ONES, TOKENS), BF16)

        for at, pair in enumerate(pairs_of):
            for chain in pair:
                fill(step, ("A2", chain), summed(receive(step, ("A1", chain))))
            keys_sent = [("A2", chain) for chain in pair]
            if at == 0:
                fill(step, ("A2", "squares"), summed(receive(step, ("A1", "squares"))))
                keys_sent.append(("A2", "squares"))
            send(step, *keys_sent)
        fill(step, ("A2", "k"), summed(receive(step, ("A1", "k"))))
        fill(step, ("A2", "v"), summed(receive(step, ("A1", "v"))))
        send(step, ("A2", "k"), ("A2", "v"))
        inverse = lax.rsqrt(summed(receive(step, ("A2", "squares"))) / width + EPS)
        inverse = jnp.broadcast_to(inverse, (LANES, LANES)).T[:SEQS]
        raw = jnp.concatenate([summed(receive(step, ("A2", chain))) for chain in chains], axis=0)
        query = (tiled(inverse) * raw + bias_rows[...]).astype(BF16)

        if step == 0:
            loads[10].wait()
        top = jnp.full((8, LANES), NEG, F32)
        for at in range(0, TOKENS, CHUNK):
            span = pl.ds(at, CHUNK)
            scores = dot_rows(keys[span, :], query) * scale + mask[span, :]
            scores_ref[span, :] = scores
            top = jnp.maximum(top, jnp.max(scores.reshape(CHUNK // 8, 8, LANES), axis=0))
        peak = jnp.max(top, axis=0, keepdims=True)
        bound = jnp.maximum(peak, 0.5 * NEG)
        for at in range(0, TOKENS, CHUNK):
            span = pl.ds(at, CHUNK)
            weights_ref[span, :] = jnp.exp2(scores_ref[span, :] - bound).astype(BF16)
        out_t = dot(values_t[...], weights_ref[...])
        total = out_t[HEAD:HEAD + 1]
        some = total > 0.0
        safe = jnp.where(some, total, 1.0)
        log_total = jnp.where(some, peak + jnp.log(safe) * LOG2E, NEG)
        out_t = out_t[:HEAD] * (1.0 / safe)
        for key in (("B1", "first"), ("B1", "second")):
            fill(step, key, log_total)
        for chain in chains:
            fill(step, ("B1", chain), out_t[span_of[chain]])
        for at, pair in enumerate(pairs_of):
            keys_sent = [("B1", chain) for chain in pair]
            send(step, *(keys_sent + [("B1", "first"), ("B1", "second")] if at == 0 else keys_sent))

        latest_key = (inverse * summed(receive(step, ("A2", "k"))) + bk[...].astype(F32)).astype(BF16)
        latest_value = (inverse * summed(receive(step, ("A2", "v"))) + bv[...].astype(F32)).astype(BF16)
        appended_ref[step, 0] = latest_key
        appended_ref[step, 1] = latest_value
        recent.append((latest_key, tiled(latest_value.astype(F32)).T))
        new_scores = [
            jnp.sum(jnp.where(own_seq, dot_rows(key, query), 0.0), axis=0, keepdims=True) * scale for key, _ in recent
        ]
        new_weights, new_total = weigh(new_scores)
        new_out = blend(new_weights, [value for _, value in recent])

        halves = ("first", "second")
        weights = [None, None]
        for at, pair in enumerate(pairs_of):
            for chain in pair:
                which = chain % 2
                if at == 0:
                    weights[which], log_total = weigh(receive(step, ("B1", halves[which])))
                    fill(step, ("B2", halves[which]), log_total)
                fill(step, ("B2", chain), blend(weights[which], receive(step, ("B1", chain))))
            keys_sent = [("B2", chain) for chain in pair]
            send(step, *(keys_sent + [("B2", "first"), ("B2", "second")] if at == 0 else keys_sent))
        for which in range(2):
            weights[which], _ = weigh(receive(step, ("B2", halves[which])) + [new_total])
        attended = [
            blend(weights[chain % 2], receive(step, ("B2", chain)) + [new_out[span_of[chain]]]) for chain in chains
        ]
        attended = jnp.concatenate(attended, axis=0).T.astype(BF16)
        attended = jnp.concatenate([attended[h * SEQS:(h + 1) * SEQS] for h in range(GROUP)], axis=1)
        if step == 0:
            loads[11].wait()
        fill(step, ("C", "layer"), dot(attended, wo[...]))
        send(step, ("C", "layer"))
        layer = summed(receive(step, ("C", "layer")))
        branch_ref[step] = layer.astype(BF16)
        current = (current + layer).astype(BF16).astype(F32)

    for step in range(STEPS):
        for key in STREAMS:
            others(step, key, send_sem)


def shards(
    stream, norm_gain, query_weight, query_bias, key_matrix, key_offset_bias, value_matrix, value_offset_bias,
    out_weight, key_pages, paged_values, block_table, lengths, *, width,
):
    operands = (
        stream, norm_gain.reshape(1, HEAD), query_weight, query_bias.reshape(GROUP, HEAD),
        key_matrix, key_offset_bias.reshape(1, HEAD), value_matrix, value_offset_bias.reshape(1, HEAD),
        out_weight, key_pages.reshape(TOKENS, HEAD), paged_values.reshape(TOKENS, HEAD), block_table, lengths,
    )
    anywhere = pl.BlockSpec(memory_space=pl.ANY)
    branch, appended = pl.pallas_call(
        functools.partial(kernel, width),
        out_shape=(
            jax.ShapeDtypeStruct((STEPS, SEQS, HEAD), BF16),
            jax.ShapeDtypeStruct((STEPS, 2, SEQS, HEAD), BF16),
        ),
        in_specs=[anywhere] * 12 + [pl.BlockSpec(memory_space=pltpu.SMEM)],
        out_specs=(pl.BlockSpec(memory_space=pltpu.VMEM), pl.BlockSpec(memory_space=pltpu.VMEM)),
        scratch_shapes=[pltpu.VMEM(operand.shape, operand.dtype) for operand in operands[:12]] + [
            pltpu.VMEM((HEAD + ONES, TOKENS), BF16),
            pltpu.VMEM((TOKENS, LANES), F32),
            pltpu.VMEM((LANES, HEAD), F32),
            pltpu.VMEM((TOKENS, LANES), F32),
            pltpu.VMEM((TOKENS, LANES), BF16),
            pltpu.VMEM((STEPS, COUNTS["rows"], RING, ROWS, LANES), BF16),
            pltpu.VMEM((STEPS, COUNTS["stat"], RING, 1, LANES), F32),
            pltpu.VMEM((STEPS, COUNTS["small"], RING, SEQS, HEAD), BF16),
            pltpu.SemaphoreType.DMA((12,)),
            pltpu.SemaphoreType.DMA((STEPS, len(STREAMS))),
            pltpu.SemaphoreType.DMA((STEPS, len(STREAMS))),
        ],
        compiler_params=pltpu.CompilerParams(
            collective_id=0, has_side_effects=True, vmem_limit_bytes=64 * 2**20
        ),
        cost_estimate=pl.CostEstimate(flops=400_000_000, bytes_accessed=2_000_000, transcendentals=600_000),
    )(*operands)
    return branch, appended.reshape(STEPS, 2, SEQS, 1, HEAD)


def solution(mesh):
    in_specs = (
        P(None, "pool"), P("pool"), P("pool", "tensor"), P("tensor"), P("pool", "tensor"), P("tensor"),
        P("pool", "tensor"), P("tensor"), P("tensor", "pool"), P("pool", None, "tensor", None),
        P("pool", None, "tensor", None), P(), P(),
    )
    out_specs = (P(None, None, "pool"), P(None, None, None, "tensor", None))
    width = mesh.shape["pool"] * HEAD
    return jax.shard_map(
        functools.partial(shards, width=width), mesh=mesh, in_specs=in_specs, out_specs=out_specs, check_vma=False
    )
```

```python
import functools
import math

import jax
import jax.numpy as jnp
from jax import lax
from jax.experimental import pallas as pl
from jax.experimental.pallas import tpu as pltpu
from jax.sharding import PartitionSpec as P

MESH = pl.DeviceIdType.MESH
EPS = 1e-06
NEG = -1e30
STEPS = 2
SEQS = 16
GROUP = 8
HEAD = 128
RING = 8
PAGE = 128
SLOTS = 16
LANES = GROUP * SEQS
TOKENS = SLOTS * PAGE
ONES = 16
SHARE = SEQS // RING
CHUNK = 256
LOG2E = math.log2(math.e)
FAR_FIRST = (4, 3, 5, 2, 6, 1, 7)
BF16 = jnp.bfloat16
F32 = jnp.float32

PAIRS = 2
ROWS = HEAD // (2 * PAIRS)
RINGS = "yz"
PHASES = ("A1", "A2", "B1", "B2")


def all_streams():
    streams = {}
    for phase in PHASES:
        for chain in range(2 * PAIRS):
            streams[phase, chain] = ("rows", RINGS[(chain + PHASES.index(phase)) % 2])
    streams["C", "layer"] = ("small", "t")
    for phase, ring in (("A1", "y"), ("A2", "z"), ("B1", "y")):
        streams[phase, "kv"] = ("kv", ring)
    for phase, name, ring in (
        ("A1", "squares", "y"), ("A2", "squares", "z"),
        ("B1", "first", "y"), ("B1", "second", "z"), ("B2", "first", "z"), ("B2", "second", "y"),
    ):
        streams[phase, name] = ("stat", ring)
    kinds = {"rows": 0, "small": 0, "stat": 0, "kv": 0}
    placed = {}
    for at, (key, (kind, ring)) in enumerate(streams.items()):
        placed[key] = (kind, kinds[kind], ring, at)
        kinds[kind] += 1
    return placed, kinds


STREAMS, COUNTS = all_streams()


def dot(a, b):
    return jnp.dot(a, b, preferred_element_type=F32)


def dot_rows(a, b):
    return lax.dot_general(a, b, (((1,), (1,)), ((), ())), preferred_element_type=F32)


def kernel(
    width,
    x_hbm, gain_hbm, wq_hbm, bq_hbm, wk_hbm, bk_hbm, wv_hbm, bv_hbm, wo_hbm, keys_hbm, values_hbm, table_hbm, lengths_hbm,
    branch_hbm, appended_hbm,
    x_ref, gain_ref, wq, bq, wk, bk, wv, bv, wo, keys, values, table, lengths_ref,
    branch_ref, appended_ref,
    values_t, mask, bias_rows, scores_ref, weights_ref,
    big, stat, small, kv, kv_out,
    local_sem, out_sem, send_sem, recv_sem,
):
    pool, tensor = lax.axis_index("pool"), lax.axis_index("tensor")
    z, y = pool // RING, lax.rem(pool, RING)

    def on_ring(axis, distance):
        if axis == "y":
            return (z * RING + lax.rem(y + distance, RING), tensor)
        if axis == "z":
            return (lax.rem(z + distance, RING) * RING + y, tensor)
        return (pool, lax.rem(tensor + distance, RING))

    partners = {(axis, distance): on_ring(axis, distance) for axis in "yzt" for distance in FAR_FIRST}
    place = {"y": y, "z": z, "t": tensor}
    homes = {"rows": big, "small": small, "stat": stat, "kv": kv}

    def slots(step, key):
        kind, at, _, _ = STREAMS[key]
        return homes[kind].at[step, at]

    def fill(step, key, value):
        ref = slots(step, key)
        ref[place[STREAMS[key][2]]] = value.astype(ref.dtype)

    def send(step, *keys):
        for distance in FAR_FIRST:
            for key in keys:
                _, _, ring, at = STREAMS[key]
                own = slots(step, key).at[place[ring]]
                pltpu.make_async_remote_copy(
                    src_ref=own, dst_ref=own,
                    send_sem=send_sem.at[step, at], recv_sem=recv_sem.at[step, at],
                    device_id=partners[ring, distance], device_id_type=MESH,
                ).start()

    def scatter(step, key, pieces):
        _, _, ring, at = STREAMS[key]
        ref = slots(step, key)
        ref[place[ring]] = pieces[place[ring]]
        for distance in FAR_FIRST:
            pltpu.make_async_remote_copy(
                src_ref=pieces.at[lax.rem(place[ring] + distance, RING)], dst_ref=ref.at[place[ring]],
                send_sem=send_sem.at[step, at], recv_sem=recv_sem.at[step, at],
                device_id=partners[ring, distance], device_id_type=MESH,
            ).start()

    def others(step, key, sem):
        part = slots(step, key).at[pl.ds(0, RING - 1)]
        pltpu.make_async_copy(part, part, sem.at[step, STREAMS[key][3]]).wait()

    def receive(step, key):
        others(step, key, recv_sem)
        ref = slots(step, key)
        return [ref[i].astype(F32) for i in range(RING)]

    barrier = pltpu.get_barrier_semaphore()
    for axes in ("yz", "t"):
        for distance, axis in [(distance, axis) for distance in FAR_FIRST for axis in axes]:
            pl.semaphore_signal(barrier, inc=1, device_id=partners[axis, distance], device_id_type=MESH)

    pairs = (
        (x_hbm, x_ref), (gain_hbm, gain_ref), (wq_hbm, wq), (wk_hbm, wk), (wv_hbm, wv), (bq_hbm, bq), (bk_hbm, bk),
        (bv_hbm, bv), (table_hbm, table), (lengths_hbm, lengths_ref), (values_hbm, values), (keys_hbm, keys), (wo_hbm, wo),
    )
    loads = [pltpu.make_async_copy(src, dst, local_sem.at[at]) for at, (src, dst) in enumerate(pairs)]
    for load in loads:
        load.start()
    for load in loads[:3]:
        load.wait()

    lane = lax.broadcasted_iota(jnp.int32, (1, LANES), 1)
    lane_seq = lax.rem(lane, SEQS)
    own_seq = lax.broadcasted_iota(jnp.int32, (SEQS, LANES), 0) == lane_seq
    scale = LOG2E / math.sqrt(HEAD)

    def tiled(rows):
        return jnp.concatenate([rows] * GROUP, axis=0)

    def weigh(peaks):
        top = peaks[0]
        for peak in peaks[1:]:
            top = jnp.maximum(top, peak)
        weights = [jnp.exp2(peak - top) for peak in peaks]
        total = weights[0]
        for weight in weights[1:]:
            total = total + weight
        share = 1.0 / total
        return [weight * share for weight in weights], top + jnp.log(total) * LOG2E

    def blend(weights, parts):
        out = weights[0] * parts[0]
        for weight, part in zip(weights[1:], parts[1:]):
            out = out + weight * part
        return out

    def summed(parts):
        total = parts[0]
        for part in parts[1:]:
            total = total + part
        return total

    chains = range(2 * PAIRS)
    pairs_of = [(2 * p, 2 * p + 1) for p in range(PAIRS)]
    span_of = [slice(c * ROWS, (c + 1) * ROWS) for c in chains]

    stores = []

    def store(ref, hbm, step, which):
        stores.append(pltpu.make_async_copy(ref.at[step], hbm.at[step], out_sem.at[step, which]))
        stores[-1].start()

    current = x_ref[...].astype(F32)
    recent = []
    for step in range(STEPS):
        scaled = (current * gain_ref[...].astype(F32)).astype(BF16)
        raw = dot(scaled, wq[...]).astype(BF16)
        for chain in chains:
            own = slots(step, ("A1", chain))
            for at in range(ROWS // SEQS):
                h = chain * (ROWS // SEQS) + at
                own[place[RINGS[chain % 2]], at * SEQS:(at + 1) * SEQS, :] = raw[:, h * HEAD:(h + 1) * HEAD]
        squares = jnp.sum((current * current).T, axis=0, keepdims=True)
        fill(step, ("A1", "squares"), jnp.concatenate([squares, jnp.ones((1, LANES - SEQS), F32)], axis=1))
        if step == 0:
            pl.semaphore_wait(barrier, 3 * (RING - 1))
        for at, pair in enumerate(pairs_of):
            keys_sent = [("A1", chain) for chain in pair]
            send(step, *(keys_sent + [("A1", "squares")] if at == 0 else keys_sent))
        if step == 0:
            for load in loads[3:5]:
                load.wait()
        new_key, new_value = dot(scaled, wk[...]), dot(scaled, wv[...])
        for i in range(RING):
            kv_out[step, i, :SHARE] = new_key[i * SHARE:(i + 1) * SHARE]
            kv_out[step, i, SHARE:] = new_value[i * SHARE:(i + 1) * SHARE]
        scatter(step, ("A1", "kv"), kv_out.at[step])

        if step == 0:
            for load in loads[5:11]:
                load.wait()
            for h in range(GROUP):
                bias_rows[h * SEQS:(h + 1) * SEQS, :] = jnp.broadcast_to(bq[h:h + 1, :].astype(F32), (SEQS, HEAD))
            length_row = jnp.zeros((1, LANES), jnp.int32)
            for s in range(SEQS):
                length_row = jnp.where(lane_seq == s, lengths_ref[s], length_row)
            table_t = tiled(table[...].astype(F32)).T
            blocks = table_t.shape[0]
            left = length_row.astype(F32) - PAGE * lax.broadcasted_iota(jnp.int32, (blocks, LANES), 0).astype(F32)
            token = lax.broadcasted_iota(jnp.int32, (PAGE, LANES), 0).astype(F32)
            first_page = pool * SLOTS
            for slot in range(SLOTS):
                span = pl.ds(slot * PAGE, PAGE)
                wanted = (first_page + slot).astype(F32)
                limit = jnp.max(jnp.where(table_t == wanted, left, 0.0), axis=0, keepdims=True)
                mask[span, :] = jnp.where(token < limit, 0.0, NEG)
                values_t[:HEAD, span] = values[span, :].T
            values_t[HEAD:, :] = jnp.ones((ONES, TOKENS), BF16)

        for at, pair in enumerate(pairs_of):
            for chain in pair:
                fill(step, ("A2", chain), summed(receive(step, ("A1", chain))))
            keys_sent = [("A2", chain) for chain in pair]
            if at == 0:
                fill(step, ("A2", "squares"), summed(receive(step, ("A1", "squares"))))
                keys_sent.append(("A2", "squares"))
            send(step, *keys_sent)
        fill(step, ("A2", "kv"), summed(receive(step, ("A1", "kv"))))
        send(step, ("A2", "kv"))
        inverse = lax.rsqrt(summed(receive(step, ("A2", "squares"))) / width + EPS)
        inverse = jnp.broadcast_to(inverse, (LANES, LANES)).T[:SEQS]
        raw = jnp.concatenate([summed(receive(step, ("A2", chain))) for chain in chains], axis=0)
        query = (tiled(inverse) * raw + bias_rows[...]).astype(BF16)

        if step == 0:
            loads[11].wait()
        top = jnp.full((8, LANES), NEG, F32)
        for at in range(0, TOKENS, CHUNK):
            span = pl.ds(at, CHUNK)
            scores = dot_rows(keys[span, :], query) * scale + mask[span, :]
            scores_ref[span, :] = scores
            top = jnp.maximum(top, jnp.max(scores.reshape(CHUNK // 8, 8, LANES), axis=0))
        peak = jnp.max(top, axis=0, keepdims=True)
        bound = jnp.maximum(peak, 0.5 * NEG)
        for at in range(0, TOKENS, CHUNK):
            span = pl.ds(at, CHUNK)
            weights_ref[span, :] = jnp.exp2(scores_ref[span, :] - bound).astype(BF16)
        out_t = dot(values_t[...], weights_ref[...])
        total = out_t[HEAD:HEAD + 1]
        some = total > 0.0
        safe = jnp.where(some, total, 1.0)
        log_total = jnp.where(some, peak + jnp.log(safe) * LOG2E, NEG)
        out_t = out_t[:HEAD] * (1.0 / safe)
        for key in (("B1", "first"), ("B1", "second")):
            fill(step, key, log_total)
        for chain in chains:
            fill(step, ("B1", chain), out_t[span_of[chain]])
        for at, pair in enumerate(pairs_of):
            keys_sent = [("B1", chain) for chain in pair]
            send(step, *([("B1", "first"), ("B1", "second")] + keys_sent if at == 0 else keys_sent))

        fill(step, ("B1", "kv"), summed(receive(step, ("A2", "kv"))))
        send(step, ("B1", "kv"))

        halves = ("first", "second")
        weights = [None, None]
        for at, pair in enumerate(pairs_of):
            for chain in pair:
                which = chain % 2
                if at == 0:
                    weights[which], log_total = weigh(receive(step, ("B1", halves[which])))
                    fill(step, ("B2", halves[which]), log_total)
                fill(step, ("B2", chain), blend(weights[which], receive(step, ("B1", chain))))
            keys_sent = [("B2", chain) for chain in pair]
            send(step, *([("B2", "first"), ("B2", "second")] + keys_sent if at == 0 else keys_sent))
        parts = receive(step, ("B1", "kv"))
        latest_key = (inverse * jnp.concatenate([part[:SHARE] for part in parts], axis=0) + bk[...].astype(F32)).astype(BF16)
        latest_value = (inverse * jnp.concatenate([part[SHARE:] for part in parts], axis=0) + bv[...].astype(F32)).astype(BF16)
        appended_ref[step, 0] = latest_key
        appended_ref[step, 1] = latest_value
        store(appended_ref, appended_hbm, step, 0)
        recent.append((latest_key, tiled(latest_value.astype(F32)).T))
        new_scores = [
            jnp.sum(jnp.where(own_seq, dot_rows(key, query), 0.0), axis=0, keepdims=True) * scale for key, _ in recent
        ]
        new_weights, new_total = weigh(new_scores)
        new_out = blend(new_weights, [value for _, value in recent])

        for which in range(2):
            weights[which], _ = weigh(receive(step, ("B2", halves[which])) + [new_total])
        attended = [
            blend(weights[chain % 2], receive(step, ("B2", chain)) + [new_out[span_of[chain]]]) for chain in chains
        ]
        attended = jnp.concatenate(attended, axis=0).T.astype(BF16)
        attended = jnp.concatenate([attended[h * SEQS:(h + 1) * SEQS] for h in range(GROUP)], axis=1)
        if step == 0:
            loads[12].wait()
        fill(step, ("C", "layer"), dot(attended, wo[...]))
        send(step, ("C", "layer"))
        layer = summed(receive(step, ("C", "layer")))
        branch_ref[step] = layer.astype(BF16)
        store(branch_ref, branch_hbm, step, 1)
        current = (current + layer).astype(BF16).astype(F32)

    for made in stores:
        made.wait()
    for step in range(STEPS):
        for key in STREAMS:
            others(step, key, send_sem)


def shards(
    stream, norm_gain, query_weight, query_bias, key_matrix, key_offset_bias, value_matrix, value_offset_bias,
    out_weight, key_pages, paged_values, block_table, lengths, *, width,
):
    operands = (
        stream, norm_gain.reshape(1, HEAD), query_weight, query_bias.reshape(GROUP, HEAD),
        key_matrix, key_offset_bias.reshape(1, HEAD), value_matrix, value_offset_bias.reshape(1, HEAD),
        out_weight, key_pages.reshape(TOKENS, HEAD), paged_values.reshape(TOKENS, HEAD), block_table, lengths,
    )
    anywhere = pl.BlockSpec(memory_space=pl.ANY)
    branch, appended = pl.pallas_call(
        functools.partial(kernel, width),
        out_shape=(
            jax.ShapeDtypeStruct((STEPS, SEQS, HEAD), BF16),
            jax.ShapeDtypeStruct((STEPS, 2, SEQS, HEAD), BF16),
        ),
        in_specs=[anywhere] * 13,
        out_specs=(anywhere, anywhere),
        scratch_shapes=[pltpu.VMEM(operand.shape, operand.dtype) for operand in operands[:12]] + [
            pltpu.SMEM((SEQS,), jnp.int32),
            pltpu.VMEM((STEPS, SEQS, HEAD), BF16),
            pltpu.VMEM((STEPS, 2, SEQS, HEAD), BF16),
            pltpu.VMEM((HEAD + ONES, TOKENS), BF16),
            pltpu.VMEM((TOKENS, LANES), F32),
            pltpu.VMEM((LANES, HEAD), F32),
            pltpu.VMEM((TOKENS, LANES), F32),
            pltpu.VMEM((TOKENS, LANES), BF16),
            pltpu.VMEM((STEPS, COUNTS["rows"], RING, ROWS, LANES), BF16),
            pltpu.VMEM((STEPS, COUNTS["stat"], RING, 1, LANES), F32),
            pltpu.VMEM((STEPS, COUNTS["small"], RING, SEQS, HEAD), BF16),
            pltpu.VMEM((STEPS, COUNTS["kv"], RING, 2 * SHARE, HEAD), F32),
            pltpu.VMEM((STEPS, RING, 2 * SHARE, HEAD), F32),
            pltpu.SemaphoreType.DMA((13,)),
            pltpu.SemaphoreType.DMA((STEPS, 2)),
            pltpu.SemaphoreType.DMA((STEPS, len(STREAMS))),
            pltpu.SemaphoreType.DMA((STEPS, len(STREAMS))),
        ],
        compiler_params=pltpu.CompilerParams(
            collective_id=0, has_side_effects=True, vmem_limit_bytes=64 * 2**20
        ),
        cost_estimate=pl.CostEstimate(flops=400_000_000, bytes_accessed=2_000_000, transcendentals=600_000),
    )(*operands)
    return branch, appended.reshape(STEPS, 2, SEQS, 1, HEAD)


def solution(mesh):
    in_specs = (
        P(None, "pool"), P("pool"), P("pool", "tensor"), P("tensor"), P("pool", "tensor"), P("tensor"),
        P("pool", "tensor"), P("tensor"), P("tensor", "pool"), P("pool", None, "tensor", None),
        P("pool", None, "tensor", None), P(), P(),
    )
    out_specs = (P(None, None, "pool"), P(None, None, None, "tensor", None))
    width = mesh.shape["pool"] * HEAD
    return jax.shard_map(
        functools.partial(shards, width=width), mesh=mesh, in_specs=in_specs, out_specs=out_specs, check_vma=False
    )
```

```python
import functools
import math

import jax
import jax.numpy as jnp
from jax import lax
from jax.experimental import pallas as pl
from jax.experimental.pallas import tpu as pltpu
from jax.sharding import PartitionSpec as P

MESH = pl.DeviceIdType.MESH
EPS = 1e-06
NEG = -1e30
STEPS = 2
SEQS = 16
GROUP = 8
HEAD = 128
RING = 8
PAGE = 128
SLOTS = 16
LANES = GROUP * SEQS
TOKENS = SLOTS * PAGE
ONES = 16
HALF = HEAD // 2
SHARE = SEQS // RING
CHUNK = 256
VMEM_ASKED = 55185 * 1024
LOG2E = math.log2(math.e)
FAR_FIRST = (4, 3, 5, 2, 6, 1, 7)
FAR, NEAR = FAR_FIRST[:3], FAR_FIRST[3:]
BF16 = jnp.bfloat16
F32 = jnp.float32

PAIRS = 2
ROWS = HEAD // (2 * PAIRS)
RINGS = "yz"
PHASES = ("A1", "A2", "B1", "B2")


def all_streams():
    streams = {}
    for phase in PHASES:
        for chain in range(2 * PAIRS):
            streams[phase, chain] = ("rows", RINGS[(chain + PHASES.index(phase)) % 2])
    streams["C", "layer"] = ("small", "t")
    for phase, ring in (("A1", "y"), ("A2", "z"), ("B1", "y")):
        streams[phase, "kv"] = ("kv", ring)
    for phase, name, ring in (
        ("A1", "squares", "y"), ("A2", "squares", "z"),
        ("B1", "first", "y"), ("B1", "second", "z"), ("B2", "first", "z"), ("B2", "second", "y"),
    ):
        streams[phase, name] = ("stat", ring)
    kinds = {"rows": 0, "small": 0, "stat": 0, "kv": 0}
    placed = {}
    for at, (key, (kind, ring)) in enumerate(streams.items()):
        placed[key] = (kind, kinds[kind], ring, at)
        kinds[kind] += 1
    return placed, kinds


STREAMS, COUNTS = all_streams()


def dot(a, b):
    return jnp.dot(a, b, preferred_element_type=F32)


def dot_rows(a, b):
    return lax.dot_general(a, b, (((1,), (1,)), ((), ())), preferred_element_type=F32)


def kernel(
    width,
    x_hbm, gain_hbm, wq_hbm, bq_hbm, wk_hbm, bk_hbm, wv_hbm, bv_hbm, wo_hbm, keys_hbm, values_hbm, table_hbm, lengths_hbm,
    branch_hbm, appended_hbm,
    x_ref, gain_ref, wq, bq, wk, bk, wv, bv, wo, keys, values, table, lengths_ref,
    branch_ref, appended_ref,
    values_t, mask, bias_rows, scores_ref, weights_ref,
    big, stat, small, kv, kv_out,
    local_sem, out_sem, send_sem, recv_sem,
):
    pool, tensor = lax.axis_index("pool"), lax.axis_index("tensor")
    z, y = pool // RING, lax.rem(pool, RING)

    def on_ring(axis, distance):
        if axis == "y":
            return (z * RING + lax.rem(y + distance, RING), tensor)
        if axis == "z":
            return (lax.rem(z + distance, RING) * RING + y, tensor)
        return (pool, lax.rem(tensor + distance, RING))

    partners = {(axis, distance): on_ring(axis, distance) for axis in "yzt" for distance in FAR_FIRST}
    place = {"y": y, "z": z, "t": tensor}
    homes = {"rows": big, "small": small, "stat": stat, "kv": kv}

    def slots(step, key):
        kind, at, _, _ = STREAMS[key]
        return homes[kind].at[step, at]

    def fill(step, key, value):
        ref = slots(step, key)
        ref[place[STREAMS[key][2]]] = value.astype(ref.dtype)

    def send(step, *keys, distances=FAR_FIRST):
        for distance in distances:
            for key in keys:
                _, _, ring, at = STREAMS[key]
                own = slots(step, key).at[place[ring]]
                pltpu.make_async_remote_copy(
                    src_ref=own, dst_ref=own,
                    send_sem=send_sem.at[step, at], recv_sem=recv_sem.at[step, at],
                    device_id=partners[ring, distance], device_id_type=MESH,
                ).start()

    def scatter(step, key, pieces):
        _, _, ring, at = STREAMS[key]
        ref = slots(step, key)
        ref[place[ring]] = pieces[place[ring]]
        for distance in FAR_FIRST:
            pltpu.make_async_remote_copy(
                src_ref=pieces.at[lax.rem(place[ring] + distance, RING)], dst_ref=ref.at[place[ring]],
                send_sem=send_sem.at[step, at], recv_sem=recv_sem.at[step, at],
                device_id=partners[ring, distance], device_id_type=MESH,
            ).start()

    def others(step, key, sem):
        part = slots(step, key).at[pl.ds(0, RING - 1)]
        pltpu.make_async_copy(part, part, sem.at[step, STREAMS[key][3]]).wait()

    def receive(step, key):
        others(step, key, recv_sem)
        ref = slots(step, key)
        return [ref[i].astype(F32) for i in range(RING)]

    barrier = pltpu.get_barrier_semaphore()
    for axes in ("yz", "t"):
        for distance, axis in [(distance, axis) for distance in FAR_FIRST for axis in axes]:
            pl.semaphore_signal(barrier, inc=1, device_id=partners[axis, distance], device_id_type=MESH)

    pairs = (
        (x_hbm, x_ref), (gain_hbm, gain_ref), (wq_hbm, wq), (wk_hbm, wk), (wv_hbm, wv), (bq_hbm, bq), (bk_hbm, bk),
        (bv_hbm, bv), (table_hbm, table), (lengths_hbm, lengths_ref), (values_hbm, values), (keys_hbm, keys), (wo_hbm, wo),
    )
    loads = [pltpu.make_async_copy(src, dst, local_sem.at[at]) for at, (src, dst) in enumerate(pairs)]
    for load in loads:
        load.start()
    for load in loads[:3]:
        load.wait()

    lane = lax.broadcasted_iota(jnp.int32, (1, LANES), 1)
    lane_seq = lax.rem(lane, SEQS)
    own_seq = lax.broadcasted_iota(jnp.int32, (SEQS, LANES), 0) == lane_seq
    scale = LOG2E / math.sqrt(HEAD)

    def tiled(rows):
        return jnp.concatenate([rows] * GROUP, axis=0)

    def weigh(peaks):
        top = peaks[0]
        for peak in peaks[1:]:
            top = jnp.maximum(top, peak)
        weights = [jnp.exp2(peak - top) for peak in peaks]
        total = weights[0]
        for weight in weights[1:]:
            total = total + weight
        share = 1.0 / total
        return [weight * share for weight in weights], top + jnp.log(total) * LOG2E

    def blend(weights, parts):
        out = weights[0] * parts[0]
        for weight, part in zip(weights[1:], parts[1:]):
            out = out + weight * part
        return out

    def summed(parts):
        total = parts[0]
        for part in parts[1:]:
            total = total + part
        return total

    def send_pairs(step, phase, ahead):
        for distances in (FAR, NEAR):
            for at, pair in enumerate(pairs_of):
                send(step, *((ahead if at == 0 else []) + [(phase, chain) for chain in pair]), distances=distances)

    chains = range(2 * PAIRS)
    pairs_of = [(2 * p, 2 * p + 1) for p in range(PAIRS)]
    span_of = [slice(c * ROWS, (c + 1) * ROWS) for c in chains]

    stores = []

    def store(ref, hbm, step, which):
        stores.append(pltpu.make_async_copy(ref.at[step], hbm.at[step], out_sem.at[step, which]))
        stores[-1].start()

    current = x_ref[...].astype(F32)
    recent = []
    for step in range(STEPS):
        scaled = (current * gain_ref[...].astype(F32)).astype(BF16)
        raw = dot(scaled, wq[...]).astype(BF16)
        for chain in chains:
            own = slots(step, ("A1", chain))
            for at in range(ROWS // SEQS):
                h = chain * (ROWS // SEQS) + at
                own[place[RINGS[chain % 2]], at * SEQS:(at + 1) * SEQS, :] = raw[:, h * HEAD:(h + 1) * HEAD]
        squares = jnp.sum((current * current).T, axis=0, keepdims=True)
        fill(step, ("A1", "squares"), jnp.concatenate([squares, jnp.ones((1, LANES - SEQS), F32)], axis=1))
        if step == 0:
            pl.semaphore_wait(barrier, 3 * (RING - 1))
        send_pairs(step, "A1", [("A1", "squares")])
        if step == 0:
            for load in loads[3:5]:
                load.wait()
        new_key, new_value = dot(scaled, wk[...]), dot(scaled, wv[...])
        for i in range(RING):
            kv_out[step, i, :SHARE] = new_key[i * SHARE:(i + 1) * SHARE]
            kv_out[step, i, SHARE:] = new_value[i * SHARE:(i + 1) * SHARE]
        scatter(step, ("A1", "kv"), kv_out.at[step])

        if step == 0:
            for load in loads[5:11]:
                load.wait()
            for h in range(GROUP):
                bias_rows[h * SEQS:(h + 1) * SEQS, :] = jnp.broadcast_to(bq[h:h + 1, :].astype(F32), (SEQS, HEAD))
            length_row = jnp.zeros((1, LANES), jnp.int32)
            for s in range(SEQS):
                length_row = jnp.where(lane_seq == s, lengths_ref[s], length_row)
            table_t = tiled(table[...].astype(F32)).T
            blocks = table_t.shape[0]
            left = length_row.astype(F32) - PAGE * lax.broadcasted_iota(jnp.int32, (blocks, LANES), 0).astype(F32)
            token = lax.broadcasted_iota(jnp.int32, (PAGE, LANES), 0).astype(F32)
            first_page = pool * SLOTS
            for slot in range(SLOTS):
                span = pl.ds(slot * PAGE, PAGE)
                wanted = (first_page + slot).astype(F32)
                limit = jnp.max(jnp.where(table_t == wanted, left, 0.0), axis=0, keepdims=True)
                mask[span, :] = jnp.where(token < limit, 0.0, NEG)
                page_t = values[span, :].T
                values_t[:HALF, span] = page_t[:HALF]
                values_t[HALF + ONES:, span] = page_t[HALF:]
            values_t[HALF:HALF + ONES, :] = jnp.ones((ONES, TOKENS), BF16)

        for at, pair in enumerate(pairs_of):
            for chain in pair:
                fill(step, ("A2", chain), summed(receive(step, ("A1", chain))))
            keys_sent = [("A2", chain) for chain in pair]
            distances = FAR_FIRST[:5] if at == 0 else FAR_FIRST[:3]
            if at == 0:
                fill(step, ("A2", "squares"), summed(receive(step, ("A1", "squares"))))
                keys_sent.append(("A2", "squares"))
            send(step, *keys_sent, distances=distances)
            if at == 1:
                send(step, ("A2", 0), ("A2", 1), ("A2", "squares"), distances=FAR_FIRST[5:])
                send(step, *keys_sent, distances=FAR_FIRST[3:])
        fill(step, ("A2", "kv"), summed(receive(step, ("A1", "kv"))))
        send(step, ("A2", "kv"))
        inverse = lax.rsqrt(summed(receive(step, ("A2", "squares"))) / width + EPS)
        inverse = jnp.broadcast_to(inverse, (LANES, LANES)).T[:SEQS]
        raw = jnp.concatenate([summed(receive(step, ("A2", chain))) for chain in chains], axis=0)
        query = (tiled(inverse) * raw + bias_rows[...]).astype(BF16)

        if step == 0:
            loads[11].wait()
        top = jnp.full((8, LANES), NEG, F32)
        for at in range(0, TOKENS, CHUNK):
            span = pl.ds(at, CHUNK)
            scores = dot_rows(keys[span, :], query) * scale + mask[span, :]
            scores_ref[span, :] = scores
            top = jnp.maximum(top, jnp.max(scores.reshape(CHUNK // 8, 8, LANES), axis=0))
        peak = jnp.max(top, axis=0, keepdims=True)
        bound = jnp.maximum(peak, 0.5 * NEG)
        for at in range(0, TOKENS, CHUNK):
            span = pl.ds(at, CHUNK)
            weights_ref[span, :] = jnp.exp2(scores_ref[span, :] - bound).astype(BF16)
        out_t = dot(values_t[:HALF + ONES, :], weights_ref[...])
        total = out_t[HALF:HALF + 1]
        some = total > 0.0
        safe = jnp.where(some, total, 1.0)
        log_total = jnp.where(some, peak + jnp.log(safe) * LOG2E, NEG)
        share = 1.0 / safe
        ahead = [("B1", "first"), ("B1", "second")]
        for key in ahead:
            fill(step, key, log_total)
        for chain in pairs_of[0]:
            fill(step, ("B1", chain), out_t[span_of[chain]] * share)
        send(step, *ahead, ("B1", 0), ("B1", 1), distances=FAR)
        out_t = dot(values_t[HALF + ONES:, :], weights_ref[...])
        for chain in pairs_of[1]:
            fill(step, ("B1", chain), out_t[(chain - 2) * ROWS:(chain - 1) * ROWS] * share)
        send(step, ("B1", 2), ("B1", 3), distances=FAR)
        send(step, *ahead, ("B1", 0), ("B1", 1), distances=NEAR)
        send(step, ("B1", 2), ("B1", 3), distances=NEAR)
        fill(step, ("B1", "kv"), summed(receive(step, ("A2", "kv"))))
        send(step, ("B1", "kv"))

        halves = ("first", "second")
        weights = [None, None]
        for at, pair in enumerate(pairs_of):
            for chain in pair:
                which = chain % 2
                if at == 0:
                    weights[which], log_total = weigh(receive(step, ("B1", halves[which])))
                    fill(step, ("B2", halves[which]), log_total)
                fill(step, ("B2", chain), blend(weights[which], receive(step, ("B1", chain))))
            keys_sent = [("B2", chain) for chain in pair]
            if at == 0:
                first_sent = [("B2", "first"), ("B2", "second")] + keys_sent
                send(step, *first_sent, distances=FAR_FIRST[:5])
            else:
                send(step, *keys_sent, distances=FAR)
                send(step, *first_sent, distances=FAR_FIRST[5:])
                send(step, *keys_sent, distances=NEAR)
        parts = receive(step, ("B1", "kv"))
        latest_key = (inverse * jnp.concatenate([part[:SHARE] for part in parts], axis=0) + bk[...].astype(F32)).astype(BF16)
        latest_value = (inverse * jnp.concatenate([part[SHARE:] for part in parts], axis=0) + bv[...].astype(F32)).astype(BF16)
        appended_ref[step, 0] = latest_key
        appended_ref[step, 1] = latest_value
        store(appended_ref, appended_hbm, step, 0)
        recent.append((latest_key, tiled(latest_value.astype(F32)).T))
        new_scores = [
            jnp.sum(jnp.where(own_seq, dot_rows(key, query), 0.0), axis=0, keepdims=True) * scale for key, _ in recent
        ]
        new_weights, new_total = weigh(new_scores)
        new_out = blend(new_weights, [value for _, value in recent])

        for which in range(2):
            weights[which], _ = weigh(receive(step, ("B2", halves[which])) + [new_total])
        attended = [
            blend(weights[chain % 2], receive(step, ("B2", chain)) + [new_out[span_of[chain]]]) for chain in chains
        ]
        attended = jnp.concatenate(attended, axis=0).T.astype(BF16)
        attended = jnp.concatenate([attended[h * SEQS:(h + 1) * SEQS] for h in range(GROUP)], axis=1)
        if step == 0:
            loads[12].wait()
        fill(step, ("C", "layer"), dot(attended, wo[...]))
        send(step, ("C", "layer"))
        layer = summed(receive(step, ("C", "layer")))
        branch_ref[step] = layer.astype(BF16)
        store(branch_ref, branch_hbm, step, 1)
        current = (current + layer).astype(BF16).astype(F32)

    for made in stores:
        made.wait()
    for step in range(STEPS):
        for key in STREAMS:
            others(step, key, send_sem)


def shards(
    stream, norm_gain, query_weight, query_bias, key_matrix, key_offset_bias, value_matrix, value_offset_bias,
    out_weight, key_pages, paged_values, block_table, lengths, *, width,
):
    operands = (
        stream, norm_gain.reshape(1, HEAD), query_weight, query_bias.reshape(GROUP, HEAD),
        key_matrix, key_offset_bias.reshape(1, HEAD), value_matrix, value_offset_bias.reshape(1, HEAD),
        out_weight, key_pages.reshape(TOKENS, HEAD), paged_values.reshape(TOKENS, HEAD), block_table, lengths,
    )
    anywhere = pl.BlockSpec(memory_space=pl.ANY)
    branch, appended = pl.pallas_call(
        functools.partial(kernel, width),
        out_shape=(
            jax.ShapeDtypeStruct((STEPS, SEQS, HEAD), BF16),
            jax.ShapeDtypeStruct((STEPS, 2, SEQS, HEAD), BF16),
        ),
        in_specs=[anywhere] * 13,
        out_specs=(anywhere, anywhere),
        scratch_shapes=[pltpu.VMEM(operand.shape, operand.dtype) for operand in operands[:12]] + [
            pltpu.SMEM((SEQS,), jnp.int32),
            pltpu.VMEM((STEPS, SEQS, HEAD), BF16),
            pltpu.VMEM((STEPS, 2, SEQS, HEAD), BF16),
            pltpu.VMEM((HEAD + ONES, TOKENS), BF16),
            pltpu.VMEM((TOKENS, LANES), F32),
            pltpu.VMEM((LANES, HEAD), F32),
            pltpu.VMEM((TOKENS, LANES), F32),
            pltpu.VMEM((TOKENS, LANES), BF16),
            pltpu.VMEM((STEPS, COUNTS["rows"], RING, ROWS, LANES), BF16),
            pltpu.VMEM((STEPS, COUNTS["stat"], RING, 1, LANES), F32),
            pltpu.VMEM((STEPS, COUNTS["small"], RING, SEQS, HEAD), BF16),
            pltpu.VMEM((STEPS, COUNTS["kv"], RING, 2 * SHARE, HEAD), F32),
            pltpu.VMEM((STEPS, RING, 2 * SHARE, HEAD), F32),
            pltpu.SemaphoreType.DMA((13,)),
            pltpu.SemaphoreType.DMA((STEPS, 2)),
            pltpu.SemaphoreType.DMA((STEPS, len(STREAMS))),
            pltpu.SemaphoreType.DMA((STEPS, len(STREAMS))),
        ],
        compiler_params=pltpu.CompilerParams(
            collective_id=0, has_side_effects=True, vmem_limit_bytes=VMEM_ASKED
        ),
        cost_estimate=pl.CostEstimate(flops=400_000_000, bytes_accessed=2_000_000, transcendentals=600_000),
    )(*operands)
    return branch, appended.reshape(STEPS, 2, SEQS, 1, HEAD)


def solution(mesh):
    in_specs = (
        P(None, "pool"), P("pool"), P("pool", "tensor"), P("tensor"), P("pool", "tensor"), P("tensor"),
        P("pool", "tensor"), P("tensor"), P("tensor", "pool"), P("pool", None, "tensor", None),
        P("pool", None, "tensor", None), P(), P(),
    )
    out_specs = (P(None, None, "pool"), P(None, None, None, "tensor", None))
    width = mesh.shape["pool"] * HEAD
    return jax.shard_map(
        functools.partial(shards, width=width), mesh=mesh, in_specs=in_specs, out_specs=out_specs, check_vma=False
    )
```

```python
import functools
import math

import jax
import jax.numpy as jnp
from jax import lax
from jax.experimental import pallas as pl
from jax.experimental.pallas import tpu as pltpu
from jax.sharding import PartitionSpec as P

MESH = pl.DeviceIdType.MESH
EPS = 1e-06
NEG = -1e30
STEPS = 2
SEQS = 16
GROUP = 8
HEAD = 128
RING = 8
PAGE = 128
SLOTS = 16
LANES = GROUP * SEQS
TOKENS = SLOTS * PAGE
ONES = 16
HALF = 32
SHARE = SEQS // RING
CHUNK = 256
VMEM_ASKED = 55185 * 1024
LOG2E = math.log2(math.e)
FAR_FIRST = (4, 3, 5, 2, 6, 1, 7)
FAR, NEAR = FAR_FIRST[:3], FAR_FIRST[3:]
BF16 = jnp.bfloat16
F32 = jnp.float32

PAIRS = 2
ROWS_OF = (16, 16, 48, 48)
ROWS = max(ROWS_OF)
RINGS = "yz"
PHASES = ("A1", "A2", "B1", "B2")


def all_streams():
    streams = {}
    for phase in PHASES:
        for chain in range(2 * PAIRS):
            streams[phase, chain] = ("rows", RINGS[(chain + PHASES.index(phase)) % 2])
    streams["C", "layer"] = ("small", "t")
    for phase, ring in (("A1", "y"), ("A2", "z"), ("B1", "y")):
        streams[phase, "kv"] = ("kv", ring)
    for phase, name, ring in (
        ("A1", "squares", "y"), ("A2", "squares", "z"),
        ("B1", "first", "y"), ("B1", "second", "z"), ("B2", "first", "z"), ("B2", "second", "y"),
    ):
        streams[phase, name] = ("stat", ring)
    kinds = {"rows": 0, "small": 0, "stat": 0, "kv": 0}
    placed = {}
    for at, (key, (kind, ring)) in enumerate(streams.items()):
        placed[key] = (kind, kinds[kind], ring, at)
        kinds[kind] += 1
    return placed, kinds


STREAMS, COUNTS = all_streams()


def dot(a, b):
    return jnp.dot(a, b, preferred_element_type=F32)


def dot_rows(a, b):
    return lax.dot_general(a, b, (((1,), (1,)), ((), ())), preferred_element_type=F32)


def kernel(
    width,
    x_hbm, gain_hbm, wq_hbm, bq_hbm, wk_hbm, bk_hbm, wv_hbm, bv_hbm, wo_hbm, keys_hbm, values_hbm, table_hbm, lengths_hbm,
    branch_hbm, appended_hbm,
    x_ref, gain_ref, wq, bq, wk, bk, wv, bv, wo, keys, values, table, lengths_ref,
    branch_ref, appended_ref,
    values_t, mask, bias_rows, scores_ref, weights_ref,
    big, stat, small, kv, kv_out,
    local_sem, out_sem, send_sem, recv_sem,
):
    pool, tensor = lax.axis_index("pool"), lax.axis_index("tensor")
    z, y = pool // RING, lax.rem(pool, RING)

    def on_ring(axis, distance):
        if axis == "y":
            return (z * RING + lax.rem(y + distance, RING), tensor)
        if axis == "z":
            return (lax.rem(z + distance, RING) * RING + y, tensor)
        return (pool, lax.rem(tensor + distance, RING))

    partners = {(axis, distance): on_ring(axis, distance) for axis in "yzt" for distance in FAR_FIRST}
    place = {"y": y, "z": z, "t": tensor}
    homes = {"rows": big, "small": small, "stat": stat, "kv": kv}

    def slots(step, key):
        kind, at, _, _ = STREAMS[key]
        if kind == "rows":
            return homes[kind].at[step, at, :, pl.ds(0, ROWS_OF[key[1]])]
        return homes[kind].at[step, at]

    def fill(step, key, value):
        ref = slots(step, key)
        ref[place[STREAMS[key][2]]] = value.astype(ref.dtype)

    def send(step, *keys, distances=FAR_FIRST):
        for distance in distances:
            for key in keys:
                _, _, ring, at = STREAMS[key]
                own = slots(step, key).at[place[ring]]
                pltpu.make_async_remote_copy(
                    src_ref=own, dst_ref=own,
                    send_sem=send_sem.at[step, at], recv_sem=recv_sem.at[step, at],
                    device_id=partners[ring, distance], device_id_type=MESH,
                ).start()

    def scatter(step, key, pieces):
        _, _, ring, at = STREAMS[key]
        ref = slots(step, key)
        ref[place[ring]] = pieces[place[ring]]
        for distance in FAR_FIRST:
            pltpu.make_async_remote_copy(
                src_ref=pieces.at[lax.rem(place[ring] + distance, RING)], dst_ref=ref.at[place[ring]],
                send_sem=send_sem.at[step, at], recv_sem=recv_sem.at[step, at],
                device_id=partners[ring, distance], device_id_type=MESH,
            ).start()

    def others(step, key, sem):
        part = slots(step, key).at[pl.ds(0, RING - 1)]
        pltpu.make_async_copy(part, part, sem.at[step, STREAMS[key][3]]).wait()

    def drain(step, *phases):
        for key in STREAMS:
            if key[0] in phases:
                others(step, key, send_sem)

    def receive(step, key):
        others(step, key, recv_sem)
        ref = slots(step, key)
        return [ref[i].astype(F32) for i in range(RING)]

    barrier = pltpu.get_barrier_semaphore()
    for axes in ("yz", "t"):
        for distance, axis in [(distance, axis) for distance in FAR_FIRST for axis in axes]:
            pl.semaphore_signal(barrier, inc=1, device_id=partners[axis, distance], device_id_type=MESH)

    pairs = (
        (x_hbm, x_ref), (gain_hbm, gain_ref), (wq_hbm, wq), (wk_hbm, wk), (wv_hbm, wv), (bq_hbm, bq), (bk_hbm, bk),
        (bv_hbm, bv), (table_hbm, table), (lengths_hbm, lengths_ref), (values_hbm, values), (keys_hbm, keys), (wo_hbm, wo),
    )
    loads = [pltpu.make_async_copy(src, dst, local_sem.at[at]) for at, (src, dst) in enumerate(pairs)]
    for load in loads:
        load.start()
    for load in loads[:3]:
        load.wait()

    lane = lax.broadcasted_iota(jnp.int32, (1, LANES), 1)
    lane_seq = lax.rem(lane, SEQS)
    own_seq = lax.broadcasted_iota(jnp.int32, (SEQS, LANES), 0) == lane_seq
    scale = LOG2E / math.sqrt(HEAD)

    def tiled(rows):
        return jnp.concatenate([rows] * GROUP, axis=0)

    def weigh(peaks):
        top = peaks[0]
        for peak in peaks[1:]:
            top = jnp.maximum(top, peak)
        weights = [jnp.exp2(peak - top) for peak in peaks]
        total = weights[0]
        for weight in weights[1:]:
            total = total + weight
        share = 1.0 / total
        return [weight * share for weight in weights], top + jnp.log(total) * LOG2E

    def blend(weights, parts):
        out = weights[0] * parts[0]
        for weight, part in zip(weights[1:], parts[1:]):
            out = out + weight * part
        return out

    def summed(parts):
        total = parts[0]
        for part in parts[1:]:
            total = total + part
        return total

    def send_pairs(step, phase, ahead):
        for distances in (FAR, NEAR):
            for at, pair in enumerate(pairs_of):
                send(step, *((ahead if at == 0 else []) + [(phase, chain) for chain in pair]), distances=distances)

    chains = range(2 * PAIRS)
    pairs_of = [(2 * p, 2 * p + 1) for p in range(PAIRS)]
    span_of = [slice(sum(ROWS_OF[:c]), sum(ROWS_OF[:c + 1])) for c in chains]

    stores = []

    def store(ref, hbm, step, which):
        stores.append(pltpu.make_async_copy(ref.at[step], hbm.at[step], out_sem.at[step, which]))
        stores[-1].start()

    current = x_ref[...].astype(F32)
    recent = []
    for step in range(STEPS):
        scaled = (current * gain_ref[...].astype(F32)).astype(BF16)
        raw = dot(scaled, wq[...]).astype(BF16)
        for chain in chains:
            own = slots(step, ("A1", chain))
            for at in range(ROWS_OF[chain] // SEQS):
                h = span_of[chain].start // SEQS + at
                own[place[RINGS[chain % 2]], at * SEQS:(at + 1) * SEQS, :] = raw[:, h * HEAD:(h + 1) * HEAD]
        squares = jnp.sum((current * current).T, axis=0, keepdims=True)
        fill(step, ("A1", "squares"), jnp.concatenate([squares, jnp.ones((1, LANES - SEQS), F32)], axis=1))
        if step == 0:
            pl.semaphore_wait(barrier, 3 * (RING - 1))
        send_pairs(step, "A1", [("A1", "squares")])
        if step == 0:
            for load in loads[3:5]:
                load.wait()
        new_key, new_value = dot(scaled, wk[...]), dot(scaled, wv[...])
        for i in range(RING):
            kv_out[step, i, :SHARE] = new_key[i * SHARE:(i + 1) * SHARE]
            kv_out[step, i, SHARE:] = new_value[i * SHARE:(i + 1) * SHARE]
        scatter(step, ("A1", "kv"), kv_out.at[step])
        if step > 0:
            drain(step - 1, "C")

        if step == 0:
            for load in loads[5:11]:
                load.wait()
            for h in range(GROUP):
                bias_rows[h * SEQS:(h + 1) * SEQS, :] = jnp.broadcast_to(bq[h:h + 1, :].astype(F32), (SEQS, HEAD))
            length_row = jnp.zeros((1, LANES), jnp.int32)
            for s in range(SEQS):
                length_row = jnp.where(lane_seq == s, lengths_ref[s], length_row)
            table_t = tiled(table[...].astype(F32)).T
            blocks = table_t.shape[0]
            left = length_row.astype(F32) - PAGE * lax.broadcasted_iota(jnp.int32, (blocks, LANES), 0).astype(F32)
            token = lax.broadcasted_iota(jnp.int32, (PAGE, LANES), 0).astype(F32)
            first_page = pool * SLOTS
            for slot in range(SLOTS):
                span = pl.ds(slot * PAGE, PAGE)
                wanted = (first_page + slot).astype(F32)
                limit = jnp.max(jnp.where(table_t == wanted, left, 0.0), axis=0, keepdims=True)
                mask[span, :] = jnp.where(token < limit, 0.0, NEG)
                page_t = values[span, :].T
                values_t[:HALF, span] = page_t[:HALF]
                values_t[HALF + ONES:, span] = page_t[HALF:]
            values_t[HALF:HALF + ONES, :] = jnp.ones((ONES, TOKENS), BF16)

        for at, pair in enumerate(pairs_of):
            for chain in pair:
                fill(step, ("A2", chain), summed(receive(step, ("A1", chain))))
            keys_sent = [("A2", chain) for chain in pair]
            distances = FAR_FIRST[:5] if at == 0 else FAR_FIRST[:3]
            if at == 0:
                fill(step, ("A2", "squares"), summed(receive(step, ("A1", "squares"))))
                keys_sent.append(("A2", "squares"))
            send(step, *keys_sent, distances=distances)
            if at == 1:
                send(step, ("A2", 0), ("A2", 1), ("A2", "squares"), distances=FAR_FIRST[5:])
                send(step, *keys_sent, distances=FAR_FIRST[3:])
        fill(step, ("A2", "kv"), summed(receive(step, ("A1", "kv"))))
        send(step, ("A2", "kv"))
        inverse = lax.rsqrt(summed(receive(step, ("A2", "squares"))) / width + EPS)
        inverse = jnp.broadcast_to(inverse, (LANES, LANES)).T[:SEQS]
        raw = jnp.concatenate([summed(receive(step, ("A2", chain))) for chain in chains], axis=0)
        query = (tiled(inverse) * raw + bias_rows[...]).astype(BF16)

        if step == 0:
            loads[11].wait()
        top = jnp.full((8, LANES), NEG, F32)
        for at in range(0, TOKENS, CHUNK):
            span = pl.ds(at, CHUNK)
            scores = dot_rows(keys[span, :], query) * scale + mask[span, :]
            scores_ref[span, :] = scores
            top = jnp.maximum(top, jnp.max(scores.reshape(CHUNK // 8, 8, LANES), axis=0))
        peak = jnp.max(top, axis=0, keepdims=True)
        bound = jnp.maximum(peak, 0.5 * NEG)
        for at in range(0, TOKENS, CHUNK):
            span = pl.ds(at, CHUNK)
            weights_ref[span, :] = jnp.exp2(scores_ref[span, :] - bound).astype(BF16)
        out_t = dot(values_t[:HALF + ONES, :], weights_ref[...])
        total = out_t[HALF:HALF + 1]
        some = total > 0.0
        safe = jnp.where(some, total, 1.0)
        log_total = jnp.where(some, peak + jnp.log(safe) * LOG2E, NEG)
        share = 1.0 / safe
        ahead = [("B1", "first"), ("B1", "second")]
        for key in ahead:
            fill(step, key, log_total)
        for chain in pairs_of[0]:
            fill(step, ("B1", chain), out_t[span_of[chain]] * share)
        send(step, *ahead, ("B1", 0), ("B1", 1), distances=FAR)
        out_t = dot(values_t[HALF + ONES:, :], weights_ref[...])
        for chain in pairs_of[1]:
            fill(step, ("B1", chain), out_t[span_of[chain].start - HALF:span_of[chain].stop - HALF] * share)
        send(step, ("B1", 2), ("B1", 3), distances=FAR)
        send(step, *ahead, ("B1", 0), ("B1", 1), distances=NEAR)
        send(step, ("B1", 2), ("B1", 3), distances=NEAR)
        fill(step, ("B1", "kv"), summed(receive(step, ("A2", "kv"))))
        send(step, ("B1", "kv"))
        drain(step, "A1", "A2")

        halves = ("first", "second")
        weights = [None, None]
        for at, pair in enumerate(pairs_of):
            for chain in pair:
                which = chain % 2
                if at == 0:
                    weights[which], log_total = weigh(receive(step, ("B1", halves[which])))
                    fill(step, ("B2", halves[which]), log_total)
                fill(step, ("B2", chain), blend(weights[which], receive(step, ("B1", chain))))
            keys_sent = [("B2", chain) for chain in pair]
            if at == 0:
                first_sent = [("B2", "first"), ("B2", "second")] + keys_sent
                send(step, *first_sent, distances=FAR_FIRST[:5])
            else:
                send(step, *keys_sent, distances=FAR)
                send(step, *first_sent, distances=FAR_FIRST[5:])
                send(step, *keys_sent, distances=NEAR)
        drain(step, "B1")
        parts = receive(step, ("B1", "kv"))
        latest_key = (inverse * jnp.concatenate([part[:SHARE] for part in parts], axis=0) + bk[...].astype(F32)).astype(BF16)
        latest_value = (inverse * jnp.concatenate([part[SHARE:] for part in parts], axis=0) + bv[...].astype(F32)).astype(BF16)
        appended_ref[step, 0] = latest_key
        appended_ref[step, 1] = latest_value
        store(appended_ref, appended_hbm, step, 0)
        recent.append((latest_key, tiled(latest_value.astype(F32)).T))
        new_scores = [
            jnp.sum(jnp.where(own_seq, dot_rows(key, query), 0.0), axis=0, keepdims=True) * scale for key, _ in recent
        ]
        new_weights, new_total = weigh(new_scores)
        new_out = blend(new_weights, [value for _, value in recent])

        for which in range(2):
            weights[which], _ = weigh(receive(step, ("B2", halves[which])) + [new_total])
        attended = [
            blend(weights[chain % 2], receive(step, ("B2", chain)) + [new_out[span_of[chain]]]) for chain in chains
        ]
        attended = jnp.concatenate(attended, axis=0).T.astype(BF16)
        attended = jnp.concatenate([attended[h * SEQS:(h + 1) * SEQS] for h in range(GROUP)], axis=1)
        if step == 0:
            loads[12].wait()
        fill(step, ("C", "layer"), dot(attended, wo[...]))
        send(step, ("C", "layer"))
        drain(step, "B2")
        if step == STEPS - 1:
            for made in stores[:2]:
                made.wait()
        layer = summed(receive(step, ("C", "layer")))
        branch_ref[step] = layer.astype(BF16)
        store(branch_ref, branch_hbm, step, 1)
        current = (current + layer).astype(BF16).astype(F32)

    for made in stores[2:]:
        made.wait()
    drain(STEPS - 1, "C")


def shards(
    stream, norm_gain, query_weight, query_bias, key_matrix, key_offset_bias, value_matrix, value_offset_bias,
    out_weight, key_pages, paged_values, block_table, lengths, *, width,
):
    operands = (
        stream, norm_gain.reshape(1, HEAD), query_weight, query_bias.reshape(GROUP, HEAD),
        key_matrix, key_offset_bias.reshape(1, HEAD), value_matrix, value_offset_bias.reshape(1, HEAD),
        out_weight, key_pages.reshape(TOKENS, HEAD), paged_values.reshape(TOKENS, HEAD), block_table, lengths,
    )
    anywhere = pl.BlockSpec(memory_space=pl.ANY)
    branch, appended = pl.pallas_call(
        functools.partial(kernel, width),
        out_shape=(
            jax.ShapeDtypeStruct((STEPS, SEQS, HEAD), BF16),
            jax.ShapeDtypeStruct((STEPS, 2, SEQS, HEAD), BF16),
        ),
        in_specs=[anywhere] * 13,
        out_specs=(anywhere, anywhere),
        scratch_shapes=[pltpu.VMEM(operand.shape, operand.dtype) for operand in operands[:12]] + [
            pltpu.SMEM((SEQS,), jnp.int32),
            pltpu.VMEM((STEPS, SEQS, HEAD), BF16),
            pltpu.VMEM((STEPS, 2, SEQS, HEAD), BF16),
            pltpu.VMEM((HEAD + ONES, TOKENS), BF16),
            pltpu.VMEM((TOKENS, LANES), F32),
            pltpu.VMEM((LANES, HEAD), F32),
            pltpu.VMEM((TOKENS, LANES), F32),
            pltpu.VMEM((TOKENS, LANES), BF16),
            pltpu.VMEM((STEPS, COUNTS["rows"], RING, ROWS, LANES), BF16),
            pltpu.VMEM((STEPS, COUNTS["stat"], RING, 1, LANES), F32),
            pltpu.VMEM((STEPS, COUNTS["small"], RING, SEQS, HEAD), BF16),
            pltpu.VMEM((STEPS, COUNTS["kv"], RING, 2 * SHARE, HEAD), F32),
            pltpu.VMEM((STEPS, RING, 2 * SHARE, HEAD), F32),
            pltpu.SemaphoreType.DMA((13,)),
            pltpu.SemaphoreType.DMA((STEPS, 2)),
            pltpu.SemaphoreType.DMA((STEPS, len(STREAMS))),
            pltpu.SemaphoreType.DMA((STEPS, len(STREAMS))),
        ],
        compiler_params=pltpu.CompilerParams(
            collective_id=0, has_side_effects=True, vmem_limit_bytes=VMEM_ASKED
        ),
        cost_estimate=pl.CostEstimate(flops=400_000_000, bytes_accessed=2_000_000, transcendentals=600_000),
    )(*operands)
    return branch, appended.reshape(STEPS, 2, SEQS, 1, HEAD)


def solution(mesh):
    in_specs = (
        P(None, "pool"), P("pool"), P("pool", "tensor"), P("tensor"), P("pool", "tensor"), P("tensor"),
        P("pool", "tensor"), P("tensor"), P("tensor", "pool"), P("pool", None, "tensor", None),
        P("pool", None, "tensor", None), P(), P(),
    )
    out_specs = (P(None, None, "pool"), P(None, None, None, "tensor", None))
    width = mesh.shape["pool"] * HEAD
    return jax.shard_map(
        functools.partial(shards, width=width), mesh=mesh, in_specs=in_specs, out_specs=out_specs, check_vma=False
    )
```
